512 devices in a mesh: fiber: 32 (over z, core), row: 16 (over x, y).
Axes of the slice: x: 4, y: 4, z: 16, core: 2. Of those that a mesh axis runs over, the one named last changes fastest.
Arguments:
- deltas: float32 [32, 2048, 2048], P('fiber', 'row'), may hold values from -6 to 6
- row_sketch: float32 [2048, 320], P('row'), may hold values from -0.125 to 0.125
- slab_sketch: float32 [32, 320], P('fiber'), may hold values from -6 to 6
- core_sketch: float32 [320, 320], replicated, may hold values from -0.3125 to 0.3125
- slab_sketch_two: float32 [32, 320], P('fiber'), may hold values from -6 to 6
- ranks: int32 [2], replicated, may hold values from 160 to 320
Outputs:
- core: float32 [32, 320, 320], P('fiber', None, 'row')
The draws below stay inside these ranges and needn't reach their ends.
All inputs are finite; a program needn't handle non-finite values.
Results may differ from the reference program's by a relative error of at most 0.00028.
Values sent between devices are 32-bit elements; how exact they have to be, the bound alone decides.
A program may use at most 64 MiB of HBM per device.

```python
import jax
import jax.numpy as jnp
from jax import lax

P_SIZE = 2048
Q = 2048
S = 320
SLABS = 32


def levels(key, dims, shards, smallest, largest):
    factor_of, own = 1.0, jax.random.fold_in(key, 6)
    for dim, parts in shards:
        draws = jnp.exp(jax.random.uniform(jax.random.fold_in(own, dim), (parts,), jnp.float32, smallest / len(shards), largest / len(shards)))
        factor_of = factor_of * jnp.repeat(draws, dims[dim] // parts).reshape([-1 if axis == dim else 1 for axis in range(len(dims))])
    return factor_of


def bell_draw(key, shape, width, reach, cuts=(), held_as=jnp.bfloat16):
    level = levels(key, shape, cuts, -0.22, 0.18) if cuts else 1.0
    entries = jax.random.normal(key, shape, jnp.float32) * width * level
    return jnp.minimum(jnp.maximum(entries, -reach), reach).astype(held_as)


def setup_inputs(seed: int = 0) -> dict:
    key_of = jax.random.split(jax.random.key(seed), 7)
    return {
        "deltas": bell_draw(key_of[0], (SLABS, P_SIZE, Q), 1.0, 6.0, ((0, 32), (1, 16)), jnp.float32),
        "row_sketch": bell_draw(key_of[1], (Q, S), Q ** -0.5, 0.125, ((0, 16),), jnp.float32),
        "slab_sketch": bell_draw(key_of[2], (SLABS, S), 1.0, 6.0, ((0, 32),), jnp.float32),
        "core_sketch": bell_draw(key_of[3], (S, S), S ** -0.5, 0.3125, (), jnp.float32),
        "slab_sketch_two": bell_draw(key_of[4], (SLABS, S), 1.0, 6.0, ((0, 32),), jnp.float32),
        "ranks": jax.random.randint(key_of[5], (2,), S // 2, S + 1).astype(jnp.int32),
    }


HIGH = lax.Precision.HIGHEST

def gram_of(block):
    return jnp.dot(block.T.astype(jnp.float32), block.astype(jnp.float32), precision=HIGH, preferred_element_type=jnp.float32)

def cholesky_pass(block, gram):
    lower = jnp.linalg.cholesky(gram)
    return lax.linalg.triangular_solve(lower, block, left_side=False, lower=True, transpose_a=True)

def orthonormal(block):
    return cholesky_pass(block, gram_of(block))

def reference(deltas, row_sketch, slab_sketch, core_sketch, slab_sketch_two, ranks):
    columns = jnp.arange(S, dtype=jnp.int32)

    def add_slab(total, item):
        slab, weights = item
        return (total + jnp.dot(slab.astype(jnp.float32), row_sketch.astype(jnp.float32), precision=HIGH, preferred_element_type=jnp.float32) * weights[None, :], None)
    sketch_one, unused = lax.scan(add_slab, jnp.zeros((P_SIZE, S), jnp.float32), (deltas, slab_sketch))
    kept_one = jnp.where(columns[None, :] < ranks[0], orthonormal(sketch_one), jnp.float32(0.0))

    def project(slab):
        return jnp.dot(kept_one.T.astype(jnp.float32), slab.astype(jnp.float32), precision=HIGH, preferred_element_type=jnp.float32)
    partial_core = lax.map(project, deltas)

    def add_core(total, item):
        piece, weights = item
        mixed = jnp.dot(piece.T.astype(jnp.float32), core_sketch.astype(jnp.float32), precision=HIGH, preferred_element_type=jnp.float32)
        return (total + mixed * weights[None, :], None)
    sketch_two, unused_two = lax.scan(add_core, jnp.zeros((Q, S), jnp.float32), (partial_core, slab_sketch_two))
    kept_two = jnp.where(columns[None, :] < ranks[1], orthonormal(sketch_two), jnp.float32(0.0))

    def finish(piece):
        return jnp.dot(piece.astype(jnp.float32), kept_two.astype(jnp.float32), precision=HIGH, preferred_element_type=jnp.float32)
    return lax.map(finish, partial_core)
```

```python
import jax
import jax.numpy as jnp
from jax import lax
from jax.experimental import pallas as pl
from jax.experimental.pallas import tpu as pltpu
from jax.sharding import PartitionSpec as P

F32, BF16 = jnp.float32, jnp.bfloat16
MESH = pl.DeviceIdType.MESH
S, HALF, SUB, BLOCK = 320, 160, 80, 64
SIDE = 4
ROWS = SIDE * SIDE
CHIPS = 16
LANES = 128


def split(value):
    high = value.astype(BF16)
    return high, (value - high.astype(F32)).astype(BF16)


def dot3(left, right, contract):
    numbers = ((contract[:1], contract[1:]), ((), ()))

    def one(a, b):
        return lax.dot_general(a, b, numbers, preferred_element_type=F32)

    (ah, al), (bh, bl) = left, right
    return one(ah, bh) + (one(ah, bl) + one(al, bh))


def factor_block(rows):
    sub = lax.broadcasted_iota(jnp.int32, (8, LANES), 0)
    wide = lambda piece: jnp.broadcast_to(piece, (8, LANES))
    rows, outs = list(rows), []
    for p in range(8):
        n = 8 - p
        col = [[wide(rows[p + v][:, 8 * p + k : 8 * p + k + 1]) for k in range(8)] for v in range(n)]
        row = [wide(rows[p][k : k + 1, :]) for k in range(8)]
        a = {(i, k): wide(col[0][k][i : i + 1, :]) for k in range(8) for i in range(k, 8)}
        out = None
        for k in range(8):
            inverse = 1.0 / a[k, k]
            for j in range(k + 1, 8):
                for i in range(j, 8):
                    a[i, j] = a[i, j] - (a[i, k] * a[j, k]) * inverse
            for j in range(k + 1, 8):
                factor = a[j, k] * inverse
                row[j] = row[j] - factor * row[k]
                for v in range(1, n):
                    col[v][j] = col[v][j] - factor * col[v][k]
            scaled = row[k] * inverse
            for v in range(1, n):
                rows[p + v] = rows[p + v] - col[v][k] * scaled
            final = row[k] * lax.rsqrt(a[k, k])
            out = final if out is None else jnp.where(sub == k, final, out)
        outs.append(out)
    return outs


def cholesky_steps(first, last, g, x, done):
    lane = lax.broadcasted_iota(jnp.int32, (8, LANES), 1)
    sub = lax.broadcasted_iota(jnp.int32, (8, LANES), 0)
    width = x.shape[1]

    def step(index, carry):
        rows = [
            jnp.where(
                lane < BLOCK,
                g[8 * i : 8 * i + 8, :LANES],
                jnp.where(lane - BLOCK == sub + 8 * i, 1.0, 0.0),
            )
            for i in range(8)
        ]
        block = jnp.concatenate(factor_block(rows), axis=0)
        inverse = split(block[:, BLOCK:])
        upper = dot3(inverse, split(g[:BLOCK, :]), (1, 0))
        solved = dot3(inverse, split(x[:BLOCK, :]), (1, 0))
        done[pl.ds(pl.multiple_of(index * BLOCK, BLOCK), BLOCK), :] = solved
        rest = split(upper[:, BLOCK:S])
        rest_t = split(upper[:, BLOCK:S].T)
        g[: S - BLOCK, : S - BLOCK] = g[BLOCK:, BLOCK:S] - dot3(rest_t, rest, (1, 0))
        x[: S - BLOCK, :] = x[BLOCK:, :] - dot3(rest_t, split(solved), (1, 0))
        return carry

    lax.fori_loop(first, last, step, 0)


def kernel(
    d_ref, rs_ref, w_ref, cs_ref, w2_ref, ranks_ref, out_ref,
    d_sib, d_high, d_low, w_own, w_sib, rst, rst_high, rst_low, regrouped,
    chunks, parts, sums, ys, y_high, y_low, cs_high, cs_low, w2_col,
    g, xa, pc, mixed_in, mixed_out, xi, winv, bt_out, bt_in, bt_all, bt,
    sib_sem, gather_recv, gather_send, pass_sem, z_send, z_recv, re_send, re_recv, b_send, b_recv,
):
    fiber, me = lax.axis_index("fiber"), lax.axis_index("row")
    z, core = lax.div(fiber, 2), lax.rem(fiber, 2)
    x, y = lax.div(me, SIDE), lax.rem(me, SIDE)
    other = 1 - core
    sibling = (2 * z + other, me)

    def at(dx, dy):
        return lax.rem(x + dx + SIDE, SIDE) * SIDE + lax.rem(y + dy + SIDE, SIDE)

    def along(axis, distance):
        return at(distance, 0) if axis == 0 else at(0, distance)

    def z_peer(distance):
        return lax.rem(z + distance, CHIPS)

    def remote(src, dst, send, recv, device):
        copy = pltpu.make_async_remote_copy(
            src_ref=src, dst_ref=dst, send_sem=send, recv_sem=recv, device_id=device, device_id_type=MESH
        )
        copy.start()
        return copy

    def wait_bytes(ref, sem):
        pltpu.make_async_copy(ref, ref, sem).wait()

    peers = [sibling]
    peers += [(fiber, at(dx, dy)) for dx in range(SIDE) for dy in range(SIDE) if dx or dy]
    peers += [(2 * z_peer(e) + core, me) for e in range(1, CHIPS)]
    barrier = pltpu.get_barrier_semaphore()
    for peer in peers:
        pl.semaphore_signal(barrier, inc=1, device_id=peer, device_id_type=MESH)

    rs_t = rs_ref[...].T
    for c in range(2):

        @pl.when(core == c)
        def _():
            rst[me] = rs_t[c * HALF : (c + 1) * HALF]

    w_t = jnp.broadcast_to(w_ref[...], (LANES, S)).T
    w_own[0], w_own[1] = w_t[:HALF], w_t[HALF:]
    pl.semaphore_wait(barrier, len(peers))

    def gather(buf, which, forward=None):
        send = gather_send.at[which]

        def recv(s, j, kind):
            return gather_recv.at[which, s, j, kind]

        def push(s, slot, axis, sign, part, j, kind):
            start, size = (s * SUB, SUB) if part is None else (s * SUB + part * (SUB // 2), SUB // 2)
            ref = buf(slot, start, size)
            remote(ref, ref, send, recv(s, j, kind), (fiber, along(axis, sign)))

        def arrived(s, slot, part, j, kind):
            start, size = (s * SUB, SUB) if part is None else (s * SUB + part * (SUB // 2), SUB // 2)
            wait_bytes(buf(slot, start, size), recv(s, j, kind))

        def place(s, i1, i2):
            return at(i1, i2) if s == 0 else at(i2, i1)

        offsets = (0, -1, 1, 2)

        def both(s, axis, slot, j):
            push(s, slot, axis, 1, None, j, 0)
            push(s, slot, axis, -1, None, j, 1)

        def done(s, i1, i2):
            if forward is not None:
                forward(s, place(s, i1, i2))

        for s in range(2):
            both(s, s, place(s, 0, 0), 0)
        for s in range(2):
            both(s, 1 - s, place(s, 0, 0), 1)
        for s in range(2):
            done(s, 0, 0)
        for kind, sign in ((0, 1), (1, -1)):
            for s in range(2):
                slot = place(s, -sign, 0)
                arrived(s, slot, None, 0, kind)
                push(s, slot, s, sign, kind, 0, 2 + kind)
                both(s, 1 - s, slot, 2 + kind)
                done(s, -sign, 0)
        for kind, sign in ((0, 1), (1, -1)):
            for s in range(2):
                slot = place(s, 0, -sign)
                arrived(s, slot, None, 1, kind)
                push(s, slot, 1 - s, sign, kind, 1, 2 + kind)
                done(s, 0, -sign)
        for s in range(2):
            slot = place(s, 2, 0)
            for kind in range(2):
                arrived(s, slot, kind, 0, 2 + kind)
            both(s, 1 - s, slot, 4)
            done(s, 2, 0)
        for j in (2, 3, 4):
            for kind, sign in ((0, 1), (1, -1)):
                for s in range(2):
                    slot = place(s, offsets[j - 1], -sign)
                    arrived(s, slot, None, j, kind)
                    push(s, slot, 1 - s, sign, kind, j, 2 + kind)
                    done(s, offsets[j - 1], -sign)
        for j in (1, 2, 3, 4):
            for s in range(2):
                slot = place(s, offsets[j - 1], 2)
                for kind in range(2):
                    arrived(s, slot, kind, j, 2 + kind)
                done(s, offsets[j - 1], 2)

    def fiber_sum(value, which):
        for i in range(CHIPS):
            chunks[which, i] = value[10 * i : 10 * i + 10]
        sent, got = z_send.at[which], z_recv.at[which]
        for e in range(1, CHIPS):
            to = z_peer(e)
            remote(chunks.at[which, to], parts.at[which, z], sent.at[0], got.at[0], (2 * to + core, me))
        parts[which, z] = chunks[which, z]
        wait_bytes(parts.at[which, pl.ds(0, CHIPS - 1)], got.at[0])
        total = parts[which, 0]
        for i in range(1, CHIPS):
            total = total + parts[which, i]
        sums[which, z] = total
        for e in range(1, CHIPS):
            to = z_peer(e)
            remote(sums.at[which, z], sums.at[which, z], sent.at[1], got.at[1], (2 * to + core, me))
        wait_bytes(sums.at[which, pl.ds(0, CHIPS - 1)], got.at[1])
        return jnp.concatenate([sums[which, i] for i in range(CHIPS)], axis=0)

    to_sibling = [
        remote(d_ref.at[0], d_sib, sib_sem.at[0, 0], sib_sem.at[1, 0], sibling),
        remote(w_own.at[other], w_sib, sib_sem.at[0, 1], sib_sem.at[1, 1], sibling),
    ]
    gather(lambda slot, start, size: rst.at[slot, pl.ds(start, size)], 0)
    for dx in range(SIDE):
        for dy in range(SIDE):
            if dx or dy:
                to = at(dx, dy)
                remote(
                    d_ref.at[0, :, pl.ds(pl.multiple_of(to * LANES, LANES), LANES)],
                    regrouped.at[me], re_send, re_recv, (fiber, to),
                )
    cs_high[...], cs_low[...] = split(cs_ref[...].T)
    w2_col[...] = jnp.broadcast_to(w2_ref[...], (LANES, S)).T
    d_high[:LANES], d_low[:LANES] = split(d_ref[0])
    for j in range(ROWS):
        rst_high[:, j * LANES : (j + 1) * LANES], rst_low[:, j * LANES : (j + 1) * LANES] = split(rst[j])
    regrouped[me] = d_ref[0, :, pl.ds(pl.multiple_of(me * LANES, LANES), LANES)]
    for copy in to_sibling:
        copy.wait_recv()
    d_high[LANES:], d_low[LANES:] = split(d_sib[...])
    both_slabs = dot3((rst_high[...], rst_low[...]), (d_high[...], d_low[...]), (1, 1))
    one = fiber_sum(both_slabs[:, :LANES] * w_own[core] + both_slabs[:, LANES:] * w_sib[...], 0)

    def gather_sketch(which, value):
        buf = ys.at[which]
        buf[me, core] = value

        def forward(s, slot):
            ref = buf.at[slot, core, pl.ds(s * SUB, SUB)]
            remote(ref, ref, pass_sem.at[0, which], pass_sem.at[1, which], sibling)

        gather(lambda slot, start, size: buf.at[slot, core, pl.ds(start, size)], 1 + which, forward)
        wait_bytes(buf.at[:, other], pass_sem.at[1, which])
        for j in range(ROWS):
            block = buf[j].reshape(S, LANES)
            y_high[:, j * LANES : (j + 1) * LANES], y_low[:, j * LANES : (j + 1) * LANES] = split(block)
        pair = (y_high[...], y_low[...])
        g[...] = dot3(pair, pair, (1, 1))
        return pair

    pair = gather_sketch(0, one)
    wait_bytes(regrouped.at[pl.ds(0, ROWS - 1)], re_recv)
    xa[...] = dot3(pair, split(regrouped[...].reshape(ROWS * LANES, LANES)), (1, 0))
    cholesky_steps(0, S // BLOCK, g, xa, pc)
    index = lax.broadcasted_iota(jnp.int32, (S, LANES), 0)
    pc[...] = jnp.where(index < ranks_ref[0], pc[...], 0.0)

    pc_pair = split(pc[...])
    mixed = dot3((cs_high[...], cs_low[...]), pc_pair, (1, 0)) * w2_col[...]
    mixed_out[0], mixed_out[1] = mixed[:HALF], mixed[HALF:]
    exchange = remote(mixed_out.at[other], mixed_in, sib_sem.at[0, 2], sib_sem.at[1, 2], sibling)
    exchange.wait_recv()
    to_sibling.append(exchange)
    gather_sketch(1, fiber_sum(mixed_out[core] + mixed_in[...], 1))

    local_two = split(ys[1, me].reshape(S, LANES))
    bt_part = dot3(local_two, pc_pair, (1, 1))
    for j in range(ROWS):
        bt_out[j] = bt_part[20 * j : 20 * j + 20]
    for dx in range(SIDE):
        for dy in range(SIDE):
            if dx or dy:
                to = at(dx, dy)
                remote(bt_out.at[to], bt_in.at[me], b_send.at[0], b_recv.at[0], (fiber, to))
    bt_in[me] = bt_out[me]
    square = (S, S)
    xi[...] = jnp.where(
        lax.broadcasted_iota(jnp.int32, square, 0) == lax.broadcasted_iota(jnp.int32, square, 1), 1.0, 0.0
    )
    cholesky_steps(0, 2, g, xi, winv)
    wait_bytes(bt_in.at[pl.ds(0, ROWS - 1)], b_recv.at[0])
    total = bt_in[0]
    for j in range(1, ROWS):
        total = total + bt_in[j]
    bt_all[me] = total
    for dx in range(SIDE):
        for dy in range(SIDE):
            if dx or dy:
                to = at(dx, dy)
                remote(bt_all.at[me], bt_all.at[me], b_send.at[1], b_recv.at[1], (fiber, to))
    cholesky_steps(2, S // BLOCK, g, xi, winv)
    wait_bytes(bt_all.at[pl.ds(0, ROWS - 1)], b_recv.at[1])
    for j in range(ROWS):
        bt[20 * j : 20 * j + 20, :] = bt_all[j]
        bt_out_row = winv[20 * j : 20 * j + 20, :]
        bt_in[j] = bt_out_row
    mine = bt_in[me]
    keep = lax.broadcasted_iota(jnp.int32, mine.shape, 0) + 20 * me < ranks_ref[1]
    mine = jnp.where(keep, mine, 0.0)
    core_t = dot3(split(mine), split(bt[...]), (1, 0))
    out_ref[0] = core_t.T

    for copy in to_sibling:
        copy.wait_send()
    for which in range(3):
        wait_bytes(rst.at[pl.ds(0, ROWS - 1)], gather_send.at[which])
    for which in range(2):
        wait_bytes(ys.at[which, :, core], pass_sem.at[0, which])
        for i in range(2):
            wait_bytes(parts.at[which, pl.ds(0, CHIPS - 1)], z_send.at[which, i])
    wait_bytes(regrouped.at[pl.ds(0, ROWS - 1)], re_send)
    for i in range(2):
        wait_bytes(bt_in.at[pl.ds(0, ROWS - 1)], b_send.at[i])


def local(deltas, row_sketch, slab_sketch, core_sketch, slab_sketch_two, ranks):
    vmem = lambda *shape: pltpu.VMEM(shape, F32)
    half = lambda *shape: pltpu.VMEM(shape, BF16)
    dma = pltpu.SemaphoreType.DMA
    in_vmem = pl.BlockSpec(memory_space=pltpu.VMEM)
    return pl.pallas_call(
        kernel,
        out_shape=jax.ShapeDtypeStruct((1, S, S // ROWS), F32),
        in_specs=[in_vmem] * 5 + [pl.BlockSpec(memory_space=pltpu.SMEM)],
        out_specs=in_vmem,
        scratch_shapes=[
            vmem(LANES, 2048),
            half(2 * LANES, 2048), half(2 * LANES, 2048),
            vmem(2, HALF, LANES), vmem(HALF, LANES),
            vmem(ROWS, HALF, LANES), half(HALF, 2048), half(HALF, 2048),
            vmem(ROWS, LANES, LANES),
            vmem(2, CHIPS, 10, LANES), vmem(2, CHIPS, 10, LANES), vmem(2, CHIPS, 10, LANES),
            vmem(2, ROWS, 2, HALF, LANES),
            half(S, 2048), half(S, 2048),
            half(S, S), half(S, S), vmem(S, LANES),
            vmem(S, S), vmem(S, LANES), vmem(S, LANES),
            vmem(HALF, LANES), vmem(2, HALF, LANES),
            vmem(S, S), vmem(S, S),
            vmem(ROWS, 20, S), vmem(ROWS, 20, S), vmem(ROWS, 20, S), vmem(S, S),
            dma((2, 3)),
            dma((3, 2, 5, 4)), dma((3,)),
            dma((2, 2)),
            dma((2, 2)), dma((2, 2)),
            dma(()), dma(()),
            dma((2,)), dma((2,)),
        ],
        compiler_params=pltpu.CompilerParams(
            collective_id=0, has_side_effects=True, vmem_limit_bytes=48 * 2**20
        ),
        cost_estimate=pl.CostEstimate(flops=2 * 10**9, bytes_accessed=4 * 10**6, transcendentals=0),
    )(deltas, row_sketch, slab_sketch, core_sketch, slab_sketch_two, ranks)


def solution(mesh):
    in_specs = (
        P("fiber", "row", None),
        P("row", None),
        P("fiber", None),
        P(),
        P("fiber", None),
        P(),
    )
    out_specs = P("fiber", None, "row")
    return jax.shard_map(local, mesh=mesh, in_specs=in_specs, out_specs=out_specs, check_vma=False)
```

```python
import jax
import jax.numpy as jnp
from jax import lax
from jax.experimental import pallas as pl
from jax.experimental.pallas import tpu as pltpu
from jax.sharding import PartitionSpec as P

F32, BF16 = jnp.float32, jnp.bfloat16
MESH = pl.DeviceIdType.MESH
S, HALF, SUB, BLOCK = 320, 160, 80, 64
SIDE = 4
ROWS = SIDE * SIDE
CHIPS = 16
LANES = 128
CROSS = [(0, 0), (1, 0), (3, 0), (0, 1), (0, 3), (2, 0), (0, 2)]
DIAGONAL = [(1, 1), (1, 3), (3, 1), (3, 3)]
FAR = [(1, 2), (3, 2), (2, 1), (2, 3), (2, 2)]
GROUPS = [CROSS, DIAGONAL, FAR]
OTHERS = [offset for group in GROUPS[::-1] for offset in group[::-1] if offset != (0, 0)]
AWAY = [8, 7, 9, 6, 10, 5, 11, 4, 12, 3, 13, 2, 14, 1, 15]


def split(value):
    high = value.astype(BF16)
    return high, (value - high.astype(F32)).astype(BF16)


def dot3(left, right, contract):
    numbers = ((contract[:1], contract[1:]), ((), ()))

    def one(a, b):
        return lax.dot_general(a, b, numbers, preferred_element_type=F32)

    (ah, al), (bh, bl) = left, right
    return one(ah, bh) + (one(ah, bl) + one(al, bh))


def stack3(left, right, contract):
    (ah, al), (bh, bl) = left, right
    return lax.dot_general(
        jnp.concatenate([ah, ah, al], axis=contract[0]),
        jnp.concatenate([bh, bl, bh], axis=contract[1]),
        (((contract[0],), (contract[1],)), ((), ())),
        preferred_element_type=F32,
    )


def factor_block(rows):
    sub = lax.broadcasted_iota(jnp.int32, (8, LANES), 0)

    def wide(piece):
        return jnp.broadcast_to(piece, (8, LANES))

    def lane_of(array, lane):
        return jnp.take_along_axis(array, jnp.full((8, LANES), lane, jnp.int32), axis=1)

    rows, outs = list(rows), []
    for p in range(8):
        row = [wide(rows[p][k : k + 1, :]) for k in range(8)]
        own = [lane_of(rows[p], 8 * p + k) for k in range(8)]
        a = {(i, k): wide(own[k][i : i + 1, :]) for k in range(8) for i in range(k, 8)}
        col = [lane_of(rows[p + 1], 8 * p + k) for k in range(8)] if p < 7 else None
        out = None
        for k in range(8):
            inverse = 1.0 / a[k, k]
            for j in range(k + 1, 8):
                factor = a[j, k] * inverse
                for i in range(j, 8):
                    a[i, j] = a[i, j] - a[i, k] * factor
                row[j] = row[j] - factor * row[k]
                if col:
                    col[j] = col[j] - factor * col[k]
            if col:
                rows[p + 1] = rows[p + 1] - col[k] * (row[k] * inverse)
            final = row[k] * lax.rsqrt(a[k, k])
            out = final if out is None else jnp.where(sub == k, final, out)
        outs.append(out)
        if p < 6:
            high = out.astype(BF16).astype(F32)
            low = out - high
            left = jnp.concatenate([high, high, low], axis=0)[:, :BLOCK].astype(BF16)
            right = jnp.concatenate([high, low, high], axis=0).astype(BF16)
            update = lax.dot_general(left, right, (((0,), (0,)), ((), ())), preferred_element_type=F32)
            for i in range(p + 2, 8):
                rows[i] = rows[i] - update[8 * i : 8 * i + 8]
    return outs


def cholesky_inverse(g, x, done, beside):
    lane = lax.broadcasted_iota(jnp.int32, (8, LANES), 1)
    sub = lax.broadcasted_iota(jnp.int32, (8, LANES), 0)

    def step(index, carry):
        beside(index)
        rows = [
            jnp.where(
                lane < BLOCK,
                g[8 * i : 8 * i + 8, :LANES],
                jnp.where(lane - BLOCK == sub + 8 * i, 1.0, 0.0),
            )
            for i in range(8)
        ]
        block = jnp.concatenate(factor_block(rows), axis=0)
        inverse = split(block[:, BLOCK:])
        upper = stack3(inverse, split(g[:BLOCK, :]), (1, 0))
        solved = stack3(inverse, split(x[:BLOCK, :]), (1, 0))
        done[pl.ds(pl.multiple_of(index * BLOCK, BLOCK), BLOCK), :] = solved
        rest = split(upper[:, BLOCK:])
        g[: S - BLOCK, : S - BLOCK] = g[BLOCK:, BLOCK:] - stack3(rest, rest, (0, 0))
        x[: S - BLOCK, :] = x[BLOCK:, :] - stack3(rest, split(solved), (0, 0))
        return carry

    lax.fori_loop(0, S // BLOCK, step, 0)


def kernel(
    d_hbm, rs_hbm, w_ref, cs_hbm, w2_ref, ranks_ref, out_ref,
    d_own, d_sib, d_high, d_low, w_own, w_sib, rst, rst_high, rst_low, regrouped, cs_ref,
    chunks, parts, sums, ys, y_high, y_low, cs_high, cs_low, w2_col,
    g, pc, mixed_in, mixed_out, xi, winv, bt_out, bt_in, bt_all, bt, first_sum,
    g_out, g_in, g_all, w_rows,
    in_sem, sib_sem, gather_recv, gather_send, pass_send, pass_recv,
    z_send, z_recv, re_send, re_recv, b_send, b_recv, own_sem, g_send, g_recv,
):
    fiber, me = lax.axis_index("fiber"), lax.axis_index("row")
    z, core = lax.div(fiber, 2), lax.rem(fiber, 2)
    x, y = lax.div(me, SIDE), lax.rem(me, SIDE)
    other = 1 - core
    sibling = (2 * z + other, me)
    closing = []

    def at(dx, dy):
        return lax.rem(x + dx + SIDE, SIDE) * SIDE + lax.rem(y + dy + SIDE, SIDE)

    def z_peer(distance):
        return lax.rem(z + distance, CHIPS)

    def remote(src, dst, send, recv, device):
        copy = pltpu.make_async_remote_copy(
            src_ref=src, dst_ref=dst, send_sem=send, recv_sem=recv, device_id=device, device_id_type=MESH
        )
        copy.start()
        return copy

    def wait_bytes(ref, sem):
        pltpu.make_async_copy(ref, ref, sem).wait()

    def fetch(src, dst, i):
        copy = pltpu.make_async_copy(src, dst, in_sem.at[i])
        copy.start()
        return copy

    half_of_core = pl.ds(pl.multiple_of(core * HALF, HALF), HALF)
    fetch_rs = fetch(rs_hbm.at[half_of_core], rst.at[me], 0)
    fetch_d = fetch(d_hbm.at[0], d_own, 1)
    fetch_cs = fetch(cs_hbm, cs_ref, 2)
    peers = [(2 * z_peer(e) + core, me) for e in AWAY]
    peers += [(fiber, at(dx, dy)) for dx, dy in OTHERS]
    peers += [(2 * z + other, at(dx, dy)) for dx, dy in OTHERS]
    peers += [sibling]
    barrier = pltpu.get_barrier_semaphore()
    for peer in peers:
        pl.semaphore_signal(barrier, inc=1, device_id=peer, device_id_type=MESH)
    w_t = jnp.broadcast_to(w_ref[...], (LANES, S)).T
    w_own[0], w_own[1] = w_t[:HALF], w_t[HALF:]
    fetch_rs.wait()
    fetch_d.wait()
    pl.semaphore_wait(barrier, len(peers))

    def gather(buf, which):
        send = gather_send.at[which]
        closing.append(lambda: wait_bytes(rst.at[pl.ds(0, ROWS - 1)], send))

        def piece(s, slot):
            return buf(slot, s * SUB, SUB)

        def push(s, slot, axis, j):
            for d in (2, 1, 3):
                ref = piece(s, slot)
                to = at(d, 0) if axis == 0 else at(0, d)
                remote(ref, ref, send, gather_recv.at[which, s, j, d - 1], (fiber, to))

        def arrived(s, ex, ey):
            near, last = (ex, ey) if s == 0 else (ey, ex)
            sem = gather_recv.at[which, s, 1 + near, last - 1] if last else gather_recv.at[which, s, 0, near - 1]
            slot = at(-ex, -ey)
            wait_bytes(piece(s, slot), sem)
            if not last:
                push(s, slot, 1 - s, 1 + near)

        def start():
            for s in range(2):
                push(s, me, s, 0)
            for s in range(2):
                push(s, me, 1 - s, 1)

        def first():
            for e in (1, 3, 2):
                for s in range(2):
                    arrived(s, *((e, 0) if s == 0 else (0, e)))

        def rest(offsets):
            for ex, ey in offsets:
                for s in range(2):
                    if (ex, ey)[1 - s]:
                        arrived(s, ex, ey)

        return start, first, rest

    def add_to(ref, first, value):
        ref[...] = value if first == 0 else ref[...] + value

    def fiber_sum(value, which):
        for i in range(CHIPS):
            chunks[which, i] = value[10 * i : 10 * i + 10]
        sent, got = z_send.at[which], z_recv.at[which]
        for i in range(2):
            closing.append(lambda i=i: wait_bytes(parts.at[which, pl.ds(0, CHIPS - 1)], sent.at[i]))
        for e in AWAY:
            to = z_peer(e)
            remote(chunks.at[which, to], parts.at[which, z], sent.at[0], got.at[0], (2 * to + core, me))
        parts[which, z] = chunks[which, z]
        wait_bytes(parts.at[which, pl.ds(0, CHIPS - 1)], got.at[0])
        total = parts[which, 0]
        for i in range(1, CHIPS):
            total = total + parts[which, i]
        sums[which, z] = total
        for e in AWAY:
            to = z_peer(e)
            remote(sums.at[which, z], sums.at[which, z], sent.at[1], got.at[1], (2 * to + core, me))
        wait_bytes(sums.at[which, pl.ds(0, CHIPS - 1)], got.at[1])
        return jnp.concatenate([sums[which, i] for i in range(CHIPS)], axis=0)

    to_sibling = [
        remote(d_own, d_sib, sib_sem.at[0, 0], sib_sem.at[1, 0], sibling),
        remote(w_own.at[other], w_sib, sib_sem.at[0, 1], sib_sem.at[1, 1], sibling),
    ]
    for copy in to_sibling:
        closing.append(copy.wait_send)

    def columns(slot):
        return pl.ds(pl.multiple_of(slot * LANES, LANES), LANES)

    def first_group(first, slots):
        if first == 0:
            fetch_cs.wait()
            cs_high[...], cs_low[...] = split(cs_ref[...].T)
            w2_col[...] = jnp.broadcast_to(w2_ref[...], (LANES, S)).T
            for copy in to_sibling:
                copy.wait_recv()
            i = 0
            for offsets in GROUPS:
                for ex, ey in offsets:
                    cols = columns(at(-ex, -ey))
                    here = slice(i * LANES, (i + 1) * LANES)
                    d_high[:LANES, here], d_low[:LANES, here] = split(d_own[:, cols])
                    d_high[LANES:, here], d_low[LANES:, here] = split(d_sib[:, cols])
                    i += 1
        if first + len(slots) == ROWS:
            for dx, dy in OTHERS:
                to = at(dx, dy)
                remote(d_own.at[:, columns(to)], regrouped.at[me], re_send, re_recv, (fiber, to))
            closing.append(lambda: wait_bytes(regrouped.at[pl.ds(0, ROWS - 1)], re_send))
        for i, slot in enumerate(slots):
            here = slice((first + i) * LANES, (first + i + 1) * LANES)
            rst_high[:, here], rst_low[:, here] = split(rst[slot])
        here = slice(first * LANES, (first + len(slots)) * LANES)
        add_to(
            first_sum, first, dot3((rst_high[:, here], rst_low[:, here]), (d_high[:, here], d_low[:, here]), (1, 1))
        )

    start, first, rest = gather(lambda slot, start, size: rst.at[slot, pl.ds(start, size)], 0)
    start()
    first()
    count = 0
    for offsets in GROUPS:
        rest(offsets)
        first_group(count, [at(-ex, -ey) for ex, ey in offsets])
        count += len(offsets)
    regrouped[me] = d_own[:, columns(me)]
    one = fiber_sum(first_sum[:, :LANES] * w_own[core] + first_sum[:, LANES:] * w_sib[...], 0)

    def to_pair(value, which):
        ys[which, me, core] = value
        ref = ys.at[which, me, core]
        copy = remote(ref, ref, own_sem.at[0, which], own_sem.at[1, which], sibling)
        closing.append(copy.wait_send)
        copy.wait_recv()
        return ys[which, me].reshape(S, LANES)

    def gram_sum(block, which, beside):
        high, low = split(jnp.concatenate([block, jnp.zeros((LANES // 2, LANES), F32)], axis=0))
        for c, first in ((0, 0), (1, LANES)):

            @pl.when(core == c)
            def _():
                last = LANES if c == 0 else 3 * LANES
                part = stack3((high[first:last], low[first:last]), (high[first:], low[first:]), (1, 1))
                for i in range(ROWS):
                    strip = part[8 * i : 8 * i + 8]
                    if c == 0:
                        tiles = [strip[:, LANES * t : LANES * (t + 1)] for t in range(3)]
                    else:
                        tiles = [strip[:, :LANES], strip[:, LANES:], part[LANES + 8 * i : LANES + 8 * i + 8, LANES:]]
                    for t in range(3):
                        g_out[which, i, t] = tiles[t]

        for dx, dy in OTHERS:
            to = at(dx, dy)
            remote(g_out.at[which, to], g_in.at[which, me], g_send.at[which, 0], g_recv.at[which, 0], (fiber, to))
        g_in[which, me] = g_out[which, me]
        beside[0]()
        wait_bytes(g_in.at[which, pl.ds(0, ROWS - 1)], g_recv.at[which, 0])
        total = g_in[which, 0]
        for i in range(1, ROWS):
            total = total + g_in[which, i]
        g_all[which, core, me] = total
        ref = g_all.at[which, core, me]
        for dx, dy in OTHERS:
            to = at(dx, dy)
            remote(ref, ref, g_send.at[which, 1], g_recv.at[which, 1], (fiber, to))
            remote(ref, ref, g_send.at[which, 2], g_recv.at[which, 2], (2 * z + other, to))
        remote(ref, ref, g_send.at[which, 2], g_recv.at[which, 2], sibling)
        for i in range(2):
            closing.append(lambda i=i: wait_bytes(g_in.at[which, pl.ds(0, ROWS - 1)], g_send.at[which, i]))
        closing.append(lambda: wait_bytes(g_in.at[which], g_send.at[which, 2]))
        beside[1]()
        wait_bytes(g_all.at[which, core, pl.ds(0, ROWS - 1)], g_recv.at[which, 1])
        wait_bytes(g_all.at[which, other], g_recv.at[which, 2])
        for i in range(ROWS):
            strip, under = slice(8 * i, 8 * i + 8), slice(LANES + 8 * i, LANES + 8 * i + 8)
            g[strip, :LANES] = g_all[which, 0, i, 0]
            g[strip, LANES : 2 * LANES] = g_all[which, 0, i, 1]
            g[strip, 2 * LANES :] = g_all[which, 0, i, 2][:, : LANES // 2]
            g[under, LANES : 2 * LANES] = g_all[which, 1, i, 0]
            g[under, 2 * LANES :] = g_all[which, 1, i, 1][:, : LANES // 2]
            if i < ROWS // 2:
                g[2 * LANES + 8 * i : 2 * LANES + 8 * i + 8, 2 * LANES :] = g_all[which, 1, i, 2][:, : LANES // 2]

    square = (S, S)
    identity = jnp.where(
        lax.broadcasted_iota(jnp.int32, square, 0) == lax.broadcasted_iota(jnp.int32, square, 1), 1.0, 0.0
    )
    g[...] = identity
    xi[0], xi[1] = identity, identity
    buf = ys.at[0]
    block_one = to_pair(one, 0)
    start, first, rest = gather(lambda slot, start, size: buf.at[slot, core, pl.ds(start, size)], 1)
    gram_sum(block_one, 0, (start, first))

    def pass_on(index):
        @pl.when(index == 3)
        def _():
            for offsets in GROUPS:
                rest(offsets)
            for dx, dy in OTHERS:
                ref = buf.at[at(dx, dy), core]
                remote(ref, ref, pass_send, pass_recv, sibling)

    cholesky_inverse(g, xi.at[0], winv, pass_on)
    closing.append(lambda: wait_bytes(buf.at[pl.ds(0, ROWS - 1), core], pass_send))
    wait_bytes(buf.at[pl.ds(0, ROWS - 1), other], pass_recv)
    wait_bytes(regrouped.at[pl.ds(0, ROWS - 1)], re_recv)
    for j in range(ROWS):
        here = slice(j * LANES, (j + 1) * LANES)
        y_high[:, here], y_low[:, here] = split(buf[j].reshape(S, LANES))
    slabs = split(regrouped[...].reshape(ROWS * LANES, LANES))
    projected = dot3((y_high[...], y_low[...]), slabs, (1, 0))
    index = lax.broadcasted_iota(jnp.int32, (S, LANES), 0)
    pc[...] = jnp.where(index < ranks_ref[0], dot3(split(winv[...]), split(projected), (1, 0)), 0.0)

    pc_pair = split(pc[...])
    mixed = dot3((cs_high[...], cs_low[...]), pc_pair, (1, 0)) * w2_col[...]
    mixed_out[0], mixed_out[1] = mixed[:HALF], mixed[HALF:]
    exchange = remote(mixed_out.at[other], mixed_in, sib_sem.at[0, 2], sib_sem.at[1, 2], sibling)
    closing.append(exchange.wait_send)
    exchange.wait_recv()
    block_two = to_pair(fiber_sum(mixed_out[core] + mixed_in[...], 1), 1)

    def nothing():
        pass

    def project_two():
        bt_part = dot3(split(block_two), pc_pair, (1, 1))
        for j in range(ROWS):
            bt_out[j] = bt_part[20 * j : 20 * j + 20]

    gram_sum(block_two, 1, (nothing, project_two))
    for dx, dy in OTHERS:
        to = at(dx, dy)
        remote(bt_out.at[to], bt_in.at[me], b_send.at[0], b_recv.at[0], (fiber, to))
    bt_in[me] = bt_out[me]

    def add_up(index):
        @pl.when(index == 2)
        def _():
            wait_bytes(bt_in.at[pl.ds(0, ROWS - 1)], b_recv.at[0])
            total = bt_in[0]
            for j in range(1, ROWS):
                total = total + bt_in[j]
            bt_all[me] = total
            for dx, dy in OTHERS:
                to = at(dx, dy)
                remote(bt_all.at[me], bt_all.at[me], b_send.at[1], b_recv.at[1], (fiber, to))
            for close in closing:
                close()

    cholesky_inverse(g, xi.at[1], winv, add_up)
    wait_bytes(bt_all.at[pl.ds(0, ROWS - 1)], b_recv.at[1])
    for j in range(ROWS):
        bt[20 * j : 20 * j + 20, :] = bt_all[j]
        w_rows[j] = winv[20 * j : 20 * j + 20, :]
    mine = w_rows[me]
    keep = lax.broadcasted_iota(jnp.int32, mine.shape, 0) + 20 * me < ranks_ref[1]
    mine = jnp.where(keep, mine, 0.0)
    core_t = dot3(split(mine), split(bt[...]), (1, 0))
    for i in range(S // ROWS):
        out_ref[i] = core_t[i : i + 1]
    for i in range(2):
        wait_bytes(bt_all.at[pl.ds(0, ROWS - 1)], b_send.at[i])


def local(deltas, row_sketch, slab_sketch, core_sketch, slab_sketch_two, ranks):
    vmem = lambda *shape: pltpu.VMEM(shape, F32)
    half = lambda *shape: pltpu.VMEM(shape, BF16)
    dma = pltpu.SemaphoreType.DMA
    in_vmem = pl.BlockSpec(memory_space=pltpu.VMEM)
    in_hbm = pl.BlockSpec(memory_space=pltpu.HBM)
    core_t = pl.pallas_call(
        kernel,
        out_shape=jax.ShapeDtypeStruct((S // ROWS, 1, S), F32),
        in_specs=[in_hbm, in_hbm, in_vmem, in_hbm, in_vmem, pl.BlockSpec(memory_space=pltpu.SMEM)],
        out_specs=in_vmem,
        scratch_shapes=[
            vmem(LANES, 2048), vmem(LANES, 2048),
            half(2 * LANES, 2048), half(2 * LANES, 2048),
            vmem(2, HALF, LANES), vmem(HALF, LANES),
            vmem(ROWS, HALF, LANES), half(HALF, 2048), half(HALF, 2048),
            vmem(ROWS, LANES, LANES), vmem(S, S),
            vmem(2, CHIPS, 10, LANES), vmem(2, CHIPS, 10, LANES), vmem(2, CHIPS, 10, LANES),
            vmem(2, ROWS, 2, HALF, LANES),
            half(S, 2048), half(S, 2048),
            half(S, S), half(S, S), vmem(S, LANES),
            vmem(S, S), vmem(S, LANES),
            vmem(HALF, LANES), vmem(2, HALF, LANES),
            vmem(2, S, S), vmem(S, S),
            vmem(ROWS, 20, S), vmem(ROWS, 20, S), vmem(ROWS, 20, S), vmem(S, S),
            vmem(HALF, 2 * LANES),
            vmem(2, ROWS, 3, 8, LANES), vmem(2, ROWS, 3, 8, LANES), vmem(2, 2, ROWS, 3, 8, LANES),
            vmem(ROWS, 20, S),
            dma((3,)), dma((2, 3)),
            dma((2, 2, 5, 3)), dma((2,)),
            dma(()), dma(()),
            dma((2, 2)), dma((2, 2)),
            dma(()), dma(()),
            dma((2,)), dma((2,)),
            dma((2, 2)), dma((2, 3)), dma((2, 3)),
        ],
        compiler_params=pltpu.CompilerParams(
            collective_id=0, has_side_effects=True, vmem_limit_bytes=48 * 2**20
        ),
        cost_estimate=pl.CostEstimate(flops=2 * 10**9, bytes_accessed=4 * 10**6, transcendentals=0),
    )(deltas, row_sketch.T, slab_sketch, core_sketch, slab_sketch_two, ranks)
    return jnp.transpose(core_t, (1, 2, 0))


def solution(mesh):
    in_specs = (
        P("fiber", "row", None),
        P("row", None),
        P("fiber", None),
        P(),
        P("fiber", None),
        P(),
    )
    out_specs = P("fiber", None, "row")
    return jax.shard_map(local, mesh=mesh, in_specs=in_specs, out_specs=out_specs, check_vma=False)
```

```python
import jax
import jax.numpy as jnp
from jax import lax
from jax.experimental import pallas as pl
from jax.experimental.pallas import tpu as pltpu
from jax.sharding import PartitionSpec as P

F32, BF16 = jnp.float32, jnp.bfloat16
MESH = pl.DeviceIdType.MESH
S, HALF, SUB, BLOCK = 320, 160, 80, 64
SIDE = 4
ROWS = SIDE * SIDE
CHIPS = 16
LANES = 128
CROSS = [(0, 0), (1, 0), (3, 0), (0, 1), (0, 3), (2, 0), (0, 2)]
DIAGONAL = [(1, 1), (1, 3), (3, 1), (3, 3)]
FAR = [(1, 2), (3, 2), (2, 1), (2, 3), (2, 2)]
GROUPS = [CROSS, DIAGONAL, FAR]
OTHERS = [offset for group in GROUPS[::-1] for offset in group[::-1] if offset != (0, 0)]
AWAY = [8, 7, 9, 6, 10, 5, 11, 4, 12, 3, 13, 2, 14, 1, 15]


def split(value):
    high = value.astype(BF16)
    return high, (value - high.astype(F32)).astype(BF16)


def dot3(left, right, contract):
    numbers = ((contract[:1], contract[1:]), ((), ()))

    def one(a, b):
        return lax.dot_general(a, b, numbers, preferred_element_type=F32)

    (ah, al), (bh, bl) = left, right
    return one(ah, bh) + (one(ah, bl) + one(al, bh))


def stack3(left, right, contract):
    (ah, al), (bh, bl) = left, right
    return lax.dot_general(
        jnp.concatenate([ah, ah, al], axis=contract[0]),
        jnp.concatenate([bh, bl, bh], axis=contract[1]),
        (((contract[0],), (contract[1],)), ((), ())),
        preferred_element_type=F32,
    )


def factor_block(rows):
    sub = lax.broadcasted_iota(jnp.int32, (8, LANES), 0)

    def wide(piece):
        return jnp.broadcast_to(piece, (8, LANES))

    def lane_of(array, lane):
        return jnp.take_along_axis(array, jnp.full((8, LANES), lane, jnp.int32), axis=1)

    rows, outs = list(rows), []
    for p in range(8):
        row = [wide(rows[p][k : k + 1, :]) for k in range(8)]
        own = [lane_of(rows[p], 8 * p + k) for k in range(8)]
        a = {(i, k): wide(own[k][i : i + 1, :]) for k in range(8) for i in range(k, 8)}
        col = [lane_of(rows[p + 1], 8 * p + k) for k in range(8)] if p < 7 else None
        out = None
        for k in range(8):
            inverse = 1.0 / a[k, k]
            for j in range(k + 1, 8):
                factor = a[j, k] * inverse
                for i in range(j, 8):
                    a[i, j] = a[i, j] - a[i, k] * factor
                row[j] = row[j] - factor * row[k]
                if col:
                    col[j] = col[j] - factor * col[k]
            if col:
                rows[p + 1] = rows[p + 1] - col[k] * (row[k] * inverse)
            final = row[k] * lax.rsqrt(a[k, k])
            out = final if out is None else jnp.where(sub == k, final, out)
        outs.append(out)
        if p < 6:
            high = out.astype(BF16).astype(F32)
            low = out - high
            left = jnp.concatenate([high, high, low], axis=0)[:, :BLOCK].astype(BF16)
            right = jnp.concatenate([high, low, high], axis=0).astype(BF16)
            update = lax.dot_general(left, right, (((0,), (0,)), ((), ())), preferred_element_type=F32)
            for i in range(p + 2, 8):
                rows[i] = rows[i] - update[8 * i : 8 * i + 8]
    return outs


def cholesky_inverse(g, x, done, beside, before_last):
    lane = lax.broadcasted_iota(jnp.int32, (8, LANES), 1)
    sub = lax.broadcasted_iota(jnp.int32, (8, LANES), 0)

    def step(index, last=False):
        rows = [
            jnp.where(
                lane < BLOCK,
                g[8 * i : 8 * i + 8, :LANES],
                jnp.where(lane - BLOCK == sub + 8 * i, 1.0, 0.0),
            )
            for i in range(8)
        ]
        block = jnp.concatenate(factor_block(rows), axis=0)
        inverse = split(block[:, BLOCK:])
        solved = stack3(inverse, split(x[:BLOCK, :]), (1, 0))
        if last:
            done[S - BLOCK :, :] = solved
            return
        done[pl.ds(pl.multiple_of(index * BLOCK, BLOCK), BLOCK), :] = solved
        upper = stack3(inverse, split(g[:BLOCK, :]), (1, 0))
        rest = split(upper[:, BLOCK:])
        g[: S - BLOCK, : S - BLOCK] = g[BLOCK:, BLOCK:] - stack3(rest, rest, (0, 0))
        x[: S - BLOCK, :] = x[BLOCK:, :] - stack3(rest, split(solved), (0, 0))

    def loop(index, carry):
        beside(index)
        step(index)
        return carry

    lax.fori_loop(0, S // BLOCK - 1, loop, 0)
    before_last()
    step(S // BLOCK - 1, last=True)


def kernel(
    d_hbm, rs_hbm, w_hbm, cs_hbm, w2_hbm, ranks_hbm, out_ref,
    w_ref, w2_ref, ranks_ref,
    d_own, d_sib, d_high, d_low, w_own, w_sib, rst, rst_high, rst_low, regrouped, cs_ref,
    chunks, parts, sums, ys, y_high, y_low, cs_high, cs_low, w2_col,
    g, pc, projected, mixed_in, mixed_out, own_pair, xi, winv, bt_out, bt_in, bt_all, bt, first_sum,
    g_out, g_in, g_all, w_rows,
    in_sem, sib_sem, gather_recv, gather_send, pass_send, pass_recv,
    z_send, z_recv, re_send, re_recv, b_send, b_recv, own_sem, g_send, g_recv,
):
    fiber, me = lax.axis_index("fiber"), lax.axis_index("row")
    z, core = lax.div(fiber, 2), lax.rem(fiber, 2)
    x, y = lax.div(me, SIDE), lax.rem(me, SIDE)
    other = 1 - core
    sibling = (2 * z + other, me)
    closing = []

    def at(dx, dy):
        return lax.rem(x + dx + SIDE, SIDE) * SIDE + lax.rem(y + dy + SIDE, SIDE)

    def z_peer(distance):
        return lax.rem(z + distance, CHIPS)

    def remote(src, dst, send, recv, device):
        copy = pltpu.make_async_remote_copy(
            src_ref=src, dst_ref=dst, send_sem=send, recv_sem=recv, device_id=device, device_id_type=MESH
        )
        copy.start()
        return copy

    def wait_bytes(ref, sem):
        pltpu.make_async_copy(ref, ref, sem).wait()

    def fetch(src, dst, i):
        copy = pltpu.make_async_copy(src, dst, in_sem.at[i])
        copy.start()
        return copy

    half_of_core = pl.ds(pl.multiple_of(core * HALF, HALF), HALF)
    fetch_rs = fetch(rs_hbm.at[half_of_core], rst.at[me], 0)
    fetch_d = fetch(d_hbm.at[0], d_own, 1)
    fetch_cs = fetch(cs_hbm, cs_ref, 2)
    fetch_w = fetch(w_hbm, w_ref, 3)
    fetch_later = [fetch(w2_hbm, w2_ref, 4), fetch(ranks_hbm, ranks_ref, 5)]
    peers = [(2 * z_peer(e) + core, me) for e in AWAY]
    peers += [(fiber, at(dx, dy)) for dx, dy in OTHERS]
    peers += [sibling]
    barrier = pltpu.get_barrier_semaphore()
    for peer in peers:
        pl.semaphore_signal(barrier, inc=1, device_id=peer, device_id_type=MESH)
    fetch_w.wait()
    w_t = jnp.broadcast_to(w_ref[...], (LANES, S)).T
    w_own[0], w_own[1] = w_t[:HALF], w_t[HALF:]
    fetch_rs.wait()
    fetch_d.wait()
    pl.semaphore_wait(barrier, len(peers))

    def gather(buf, which):
        send = gather_send.at[which]
        closing.append(lambda: wait_bytes(rst.at[pl.ds(0, ROWS - 1)], send))

        def piece(s, slot):
            return buf(slot, s * SUB, SUB)

        def push(s, slot, axis, j):
            for d in (2, 1, 3):
                ref = piece(s, slot)
                to = at(d, 0) if axis == 0 else at(0, d)
                remote(ref, ref, send, gather_recv.at[which, s, j, d - 1], (fiber, to))

        def arrived(s, ex, ey):
            near, last = (ex, ey) if s == 0 else (ey, ex)
            sem = gather_recv.at[which, s, 1 + near, last - 1] if last else gather_recv.at[which, s, 0, near - 1]
            slot = at(-ex, -ey)
            wait_bytes(piece(s, slot), sem)
            if not last:
                push(s, slot, 1 - s, 1 + near)

        def start():
            for s in range(2):
                push(s, me, s, 0)
            for s in range(2):
                push(s, me, 1 - s, 1)

        def first():
            for e in (1, 3, 2):
                for s in range(2):
                    arrived(s, *((e, 0) if s == 0 else (0, e)))

        def rest(offsets):
            for ex, ey in offsets:
                for s in range(2):
                    if (ex, ey)[1 - s]:
                        arrived(s, ex, ey)

        return start, first, rest

    def add_to(ref, first, value):
        ref[...] = value if first == 0 else ref[...] + value

    def fiber_sum(value, which):
        for i in range(CHIPS):
            chunks[which, i] = value[10 * i : 10 * i + 10]
        sent, got = z_send.at[which], z_recv.at[which]
        for i in range(2):
            closing.append(lambda i=i: wait_bytes(parts.at[which, pl.ds(0, CHIPS - 1)], sent.at[i]))
        for e in AWAY:
            to = z_peer(e)
            remote(chunks.at[which, to], parts.at[which, z], sent.at[0], got.at[0], (2 * to + core, me))
        parts[which, z] = chunks[which, z]
        wait_bytes(parts.at[which, pl.ds(0, CHIPS - 1)], got.at[0])
        total = parts[which, 0]
        for i in range(1, CHIPS):
            total = total + parts[which, i]
        sums[which, z] = total
        for e in AWAY:
            to = z_peer(e)
            remote(sums.at[which, z], sums.at[which, z], sent.at[1], got.at[1], (2 * to + core, me))
        wait_bytes(sums.at[which, pl.ds(0, CHIPS - 1)], got.at[1])
        return jnp.concatenate([sums[which, i] for i in range(CHIPS)], axis=0)

    to_sibling = [
        remote(d_own, d_sib, sib_sem.at[0, 0], sib_sem.at[1, 0], sibling),
        remote(w_own.at[other], w_sib, sib_sem.at[0, 1], sib_sem.at[1, 1], sibling),
    ]
    for copy in to_sibling:
        closing.append(copy.wait_send)

    def columns(slot):
        return pl.ds(pl.multiple_of(slot * LANES, LANES), LANES)

    def first_group(first, slots):
        if first == 0:
            fetch_cs.wait()
            for copy in fetch_later:
                copy.wait()
            cs_high[...], cs_low[...] = split(cs_ref[...].T)
            w2_col[...] = jnp.broadcast_to(w2_ref[...], (LANES, S)).T
            for copy in to_sibling:
                copy.wait_recv()
            i = 0
            for offsets in GROUPS:
                for ex, ey in offsets:
                    cols = columns(at(-ex, -ey))
                    here = slice(i * LANES, (i + 1) * LANES)
                    d_high[:LANES, here], d_low[:LANES, here] = split(d_own[:, cols])
                    d_high[LANES:, here], d_low[LANES:, here] = split(d_sib[:, cols])
                    i += 1
        if first + len(slots) == ROWS:
            for dx, dy in OTHERS:
                to = at(dx, dy)
                remote(d_own.at[:, columns(to)], regrouped.at[me], re_send, re_recv, (fiber, to))
            closing.append(lambda: wait_bytes(regrouped.at[pl.ds(0, ROWS - 1)], re_send))
        for i, slot in enumerate(slots):
            here = slice((first + i) * LANES, (first + i + 1) * LANES)
            rst_high[:, here], rst_low[:, here] = split(rst[slot])
        here = slice(first * LANES, (first + len(slots)) * LANES)
        add_to(
            first_sum, first, dot3((rst_high[:, here], rst_low[:, here]), (d_high[:, here], d_low[:, here]), (1, 1))
        )

    start, first, rest = gather(lambda slot, start, size: rst.at[slot, pl.ds(start, size)], 0)
    start()
    first()
    count = 0
    for offsets in GROUPS:
        rest(offsets)
        first_group(count, [at(-ex, -ey) for ex, ey in offsets])
        count += len(offsets)
    regrouped[me] = d_own[:, columns(me)]
    one = fiber_sum(first_sum[:, :LANES] * w_own[core] + first_sum[:, LANES:] * w_sib[...], 0)

    def to_pair(value, which):
        own_pair[which, core] = value
        ref = own_pair.at[which, core]
        copy = remote(ref, ref, own_sem.at[0, which], own_sem.at[1, which], sibling)
        closing.append(copy.wait_send)
        copy.wait_recv()
        return own_pair[which].reshape(S, LANES)

    def gram_sum(block, which, beside):
        high, low = split(jnp.concatenate([block, jnp.zeros((LANES // 2, LANES), F32)], axis=0))
        for c, first in ((0, 0), (1, LANES)):

            @pl.when(core == c)
            def _():
                last = LANES if c == 0 else 3 * LANES
                part = stack3((high[first:last], low[first:last]), (high[first:], low[first:]), (1, 1))
                for i in range(ROWS):
                    strip = part[8 * i : 8 * i + 8]
                    if c == 0:
                        tiles = [strip[:, LANES * t : LANES * (t + 1)] for t in range(3)]
                    else:
                        tiles = [strip[:, :LANES], strip[:, LANES:], part[LANES + 8 * i : LANES + 8 * i + 8, LANES:]]
                    for t in range(3):
                        g_out[which, i, t] = tiles[t]

        for dx, dy in OTHERS:
            to = at(dx, dy)
            remote(g_out.at[which, to], g_in.at[which, me], g_send.at[which, 0], g_recv.at[which, 0], (fiber, to))
        g_in[which, me] = g_out[which, me]
        beside[0]()
        wait_bytes(g_in.at[which, pl.ds(0, ROWS - 1)], g_recv.at[which, 0])
        total = g_in[which, 0]
        for i in range(1, ROWS):
            total = total + g_in[which, i]
        g_all[which, core, me] = total
        ref = g_all.at[which, core, me]
        for dx, dy in OTHERS:
            to = at(dx, dy)
            remote(ref, ref, g_send.at[which, 1], g_recv.at[which, 1], (fiber, to))
            remote(ref, ref, g_send.at[which, 2], g_recv.at[which, 2], (2 * z + other, to))
        remote(ref, ref, g_send.at[which, 2], g_recv.at[which, 2], sibling)
        for i in range(2):
            closing.append(lambda i=i: wait_bytes(g_in.at[which, pl.ds(0, ROWS - 1)], g_send.at[which, i]))
        closing.append(lambda: wait_bytes(g_in.at[which], g_send.at[which, 2]))
        beside[1]()
        wait_bytes(g_all.at[which, core, pl.ds(0, ROWS - 1)], g_recv.at[which, 1])
        wait_bytes(g_all.at[which, other], g_recv.at[which, 2])
        for i in range(ROWS):
            strip, under = slice(8 * i, 8 * i + 8), slice(LANES + 8 * i, LANES + 8 * i + 8)
            g[strip, :LANES] = g_all[which, 0, i, 0]
            g[strip, LANES : 2 * LANES] = g_all[which, 0, i, 1]
            g[strip, 2 * LANES :] = g_all[which, 0, i, 2][:, : LANES // 2]
            g[under, LANES : 2 * LANES] = g_all[which, 1, i, 0]
            g[under, 2 * LANES :] = g_all[which, 1, i, 1][:, : LANES // 2]
            if i < ROWS // 2:
                g[2 * LANES + 8 * i : 2 * LANES + 8 * i + 8, 2 * LANES :] = g_all[which, 1, i, 2][:, : LANES // 2]

    square = (S, S)
    identity = jnp.where(
        lax.broadcasted_iota(jnp.int32, square, 0) == lax.broadcasted_iota(jnp.int32, square, 1), 1.0, 0.0
    )
    g[...] = identity
    xi[0], xi[1] = identity, identity
    buf = ys
    block_one = to_pair(one, 0)
    ys[me] = own_pair[0]
    start, first, rest = gather(lambda slot, start, size: buf.at[slot, core, pl.ds(start, size)], 1)
    gram_sum(block_one, 0, (start, first))

    def pass_on(index):
        @pl.when(index == 1)
        def _():
            for offsets in GROUPS:
                rest(offsets)
            for dx, dy in OTHERS:
                ref = buf.at[at(dx, dy), core]
                remote(ref, ref, pass_send, pass_recv, sibling)

    def project_one():
        wait_bytes(buf.at[pl.ds(0, ROWS - 1), other], pass_recv)
        wait_bytes(regrouped.at[pl.ds(0, ROWS - 1)], re_recv)
        for j in range(ROWS):
            here = slice(j * LANES, (j + 1) * LANES)
            y_high[:, here], y_low[:, here] = split(buf[j].reshape(S, LANES))
        slabs = split(regrouped[...].reshape(ROWS * LANES, LANES))
        projected[...] = dot3((y_high[...], y_low[...]), slabs, (1, 0))

    cholesky_inverse(g, xi.at[0], winv, pass_on, project_one)
    closing.append(lambda: wait_bytes(buf.at[pl.ds(0, ROWS - 1), core], pass_send))
    index = lax.broadcasted_iota(jnp.int32, (S, LANES), 0)
    pc[...] = jnp.where(index < ranks_ref[0], dot3(split(winv[...]), split(projected[...]), (1, 0)), 0.0)

    pc_pair = split(pc[...])
    mixed = dot3((cs_high[...], cs_low[...]), pc_pair, (1, 0)) * w2_col[...]
    mixed_out[0], mixed_out[1] = mixed[:HALF], mixed[HALF:]
    exchange = remote(mixed_out.at[other], mixed_in, sib_sem.at[0, 2], sib_sem.at[1, 2], sibling)
    closing.append(exchange.wait_send)
    exchange.wait_recv()
    block_two = to_pair(fiber_sum(mixed_out[core] + mixed_in[...], 1), 1)

    def nothing():
        pass

    def project_two():
        bt_part = dot3(split(block_two), pc_pair, (1, 1))
        for j in range(ROWS):
            bt_out[j] = bt_part[20 * j : 20 * j + 20]

    gram_sum(block_two, 1, (nothing, project_two))
    for dx, dy in OTHERS:
        to = at(dx, dy)
        remote(bt_out.at[to], bt_in.at[me], b_send.at[0], b_recv.at[0], (fiber, to))
    bt_in[me] = bt_out[me]

    def add_up(index):
        @pl.when(index == 2)
        def _():
            wait_bytes(bt_in.at[pl.ds(0, ROWS - 1)], b_recv.at[0])
            total = bt_in[0]
            for j in range(1, ROWS):
                total = total + bt_in[j]
            bt_all[me] = total
            for dx, dy in OTHERS:
                to = at(dx, dy)
                remote(bt_all.at[me], bt_all.at[me], b_send.at[1], b_recv.at[1], (fiber, to))
            for close in closing:
                close()

    cholesky_inverse(g, xi.at[1], winv, add_up, nothing)
    wait_bytes(bt_all.at[pl.ds(0, ROWS - 1)], b_recv.at[1])
    for j in range(ROWS):
        bt[20 * j : 20 * j + 20, :] = bt_all[j]
        w_rows[j] = winv[20 * j : 20 * j + 20, :]
    mine = w_rows[me]
    keep = lax.broadcasted_iota(jnp.int32, mine.shape, 0) + 20 * me < ranks_ref[1]
    mine = jnp.where(keep, mine, 0.0)
    core_t = dot3(split(mine), split(bt[...]), (1, 0))
    for i in range(S // ROWS):
        out_ref[i] = core_t[i : i + 1]
    for i in range(2):
        wait_bytes(bt_all.at[pl.ds(0, ROWS - 1)], b_send.at[i])


def local(deltas, row_sketch, slab_sketch, core_sketch, slab_sketch_two, ranks):
    vmem = lambda *shape: pltpu.VMEM(shape, F32)
    half = lambda *shape: pltpu.VMEM(shape, BF16)
    dma = pltpu.SemaphoreType.DMA
    in_hbm = pl.BlockSpec(memory_space=pltpu.HBM)
    core_t = pl.pallas_call(
        kernel,
        out_shape=jax.ShapeDtypeStruct((S // ROWS, 1, S), F32),
        in_specs=[in_hbm] * 6,
        out_specs=pl.BlockSpec(memory_space=pltpu.VMEM),
        scratch_shapes=[
            vmem(1, S), vmem(1, S), pltpu.SMEM((2,), jnp.int32),
            vmem(LANES, 2048), vmem(LANES, 2048),
            half(2 * LANES, 2048), half(2 * LANES, 2048),
            vmem(2, HALF, LANES), vmem(HALF, LANES),
            vmem(ROWS, HALF, LANES), half(HALF, 2048), half(HALF, 2048),
            vmem(ROWS, LANES, LANES), vmem(S, S),
            vmem(2, CHIPS, 10, LANES), vmem(2, CHIPS, 10, LANES), vmem(2, CHIPS, 10, LANES),
            vmem(ROWS, 2, HALF, LANES),
            half(S, 2048), half(S, 2048),
            half(S, S), half(S, S), vmem(S, LANES),
            vmem(S, S), vmem(S, LANES), vmem(S, LANES),
            vmem(HALF, LANES), vmem(2, HALF, LANES), vmem(2, 2, HALF, LANES),
            vmem(2, S, S), vmem(S, S),
            vmem(ROWS, 20, S), vmem(ROWS, 20, S), vmem(ROWS, 20, S), vmem(S, S),
            vmem(HALF, 2 * LANES),
            vmem(2, ROWS, 3, 8, LANES), vmem(2, ROWS, 3, 8, LANES), vmem(2, 2, ROWS, 3, 8, LANES),
            vmem(ROWS, 20, S),
            dma((6,)), dma((2, 3)),
            dma((2, 2, 5, 3)), dma((2,)),
            dma(()), dma(()),
            dma((2, 2)), dma((2, 2)),
            dma(()), dma(()),
            dma((2,)), dma((2,)),
            dma((2, 2)), dma((2, 3)), dma((2, 3)),
        ],
        compiler_params=pltpu.CompilerParams(
            collective_id=0, has_side_effects=True, vmem_limit_bytes=62 * 2**20
        ),
        cost_estimate=pl.CostEstimate(flops=2 * 10**9, bytes_accessed=4 * 10**6, transcendentals=0),
    )(deltas, row_sketch.T, slab_sketch, core_sketch, slab_sketch_two, ranks)
    return jnp.transpose(core_t, (1, 2, 0))


def solution(mesh):
    in_specs = (
        P("fiber", "row", None),
        P("row", None),
        P("fiber", None),
        P(),
        P("fiber", None),
        P(),
    )
    out_specs = P("fiber", None, "row")
    return jax.shard_map(local, mesh=mesh, in_specs=in_specs, out_specs=out_specs, check_vma=False)
```

```python
import jax
import jax.numpy as jnp
from jax import lax
from jax.experimental import pallas as pl
from jax.experimental.pallas import tpu as pltpu
from jax.sharding import PartitionSpec as P

F32, BF16 = jnp.float32, jnp.bfloat16
MESH = pl.DeviceIdType.MESH
S, HALF, SUB, BLOCK = 320, 160, 80, 64
SIDE = 4
ROWS = SIDE * SIDE
CHIPS = 16
LANES = 128
CROSS = [(0, 0), (1, 0), (3, 0), (0, 1), (0, 3), (2, 0), (0, 2)]
DIAGONAL = [(1, 1), (1, 3), (3, 1), (3, 3)]
FAR = [(1, 2), (3, 2), (2, 1), (2, 3), (2, 2)]
GROUPS = [CROSS, DIAGONAL, FAR]
OTHERS = [offset for group in GROUPS[::-1] for offset in group[::-1] if offset != (0, 0)]
AWAY = [8, 7, 9, 6, 10, 5, 11, 4, 12, 3, 13, 2, 14, 1, 15]


def split(value):
    high = value.astype(BF16)
    return high, (value - high.astype(F32)).astype(BF16)


def dot3(left, right, contract):
    numbers = ((contract[:1], contract[1:]), ((), ()))

    def one(a, b):
        return lax.dot_general(a, b, numbers, preferred_element_type=F32)

    (ah, al), (bh, bl) = left, right
    return one(ah, bh) + (one(ah, bl) + one(al, bh))


def stack3(left, right, contract):
    (ah, al), (bh, bl) = left, right
    return lax.dot_general(
        jnp.concatenate([ah, ah, al], axis=contract[0]),
        jnp.concatenate([bh, bl, bh], axis=contract[1]),
        (((contract[0],), (contract[1],)), ((), ())),
        preferred_element_type=F32,
    )


def factor_block(rows):
    sub = lax.broadcasted_iota(jnp.int32, (8, LANES), 0)

    def wide(piece):
        return jnp.broadcast_to(piece, (8, LANES))

    def lane_of(array, lane):
        return jnp.take_along_axis(array, jnp.full((8, LANES), lane, jnp.int32), axis=1)

    rows, outs = list(rows), []
    for p in range(8):
        row = [wide(rows[p][k : k + 1, :]) for k in range(8)]
        own = [lane_of(rows[p], 8 * p + k) for k in range(8)]
        a = {(i, k): wide(own[k][i : i + 1, :]) for k in range(8) for i in range(k, 8)}
        col = [lane_of(rows[p + 1], 8 * p + k) for k in range(8)] if p < 7 else None
        out = None
        for k in range(8):
            inverse = 1.0 / a[k, k]
            for j in range(k + 1, 8):
                factor = a[j, k] * inverse
                for i in range(j, 8):
                    a[i, j] = a[i, j] - a[i, k] * factor
                row[j] = row[j] - factor * row[k]
                if col:
                    col[j] = col[j] - factor * col[k]
            if col:
                rows[p + 1] = rows[p + 1] - col[k] * (row[k] * inverse)
            final = row[k] * lax.rsqrt(a[k, k])
            out = final if out is None else jnp.where(sub == k, final, out)
        outs.append(out)
        if p < 6:
            high = out.astype(BF16).astype(F32)
            low = out - high
            left = jnp.concatenate([high, high, low], axis=0)[:, :BLOCK].astype(BF16)
            right = jnp.concatenate([high, low, high], axis=0).astype(BF16)
            update = lax.dot_general(left, right, (((0,), (0,)), ((), ())), preferred_element_type=F32)
            for i in range(p + 2, 8):
                rows[i] = rows[i] - update[8 * i : 8 * i + 8]
    return outs


def cholesky_inverse(g, x, done, beside, before_last):
    lane = lax.broadcasted_iota(jnp.int32, (8, LANES), 1)
    sub = lax.broadcasted_iota(jnp.int32, (8, LANES), 0)

    def step(index, last=False):
        rows = [
            jnp.where(
                lane < BLOCK,
                g[8 * i : 8 * i + 8, :LANES],
                jnp.where(lane - BLOCK == sub + 8 * i, 1.0, 0.0),
            )
            for i in range(8)
        ]
        block = jnp.concatenate(factor_block(rows), axis=0)
        inverse = split(block[:, BLOCK:])
        solved = stack3(inverse, split(x[:BLOCK, :]), (1, 0))
        if last:
            done[S - BLOCK :, :] = solved
            return
        done[pl.ds(pl.multiple_of(index * BLOCK, BLOCK), BLOCK), :] = solved
        upper = stack3(inverse, split(g[:BLOCK, :]), (1, 0))
        rest = split(upper[:, BLOCK:])
        g[: S - BLOCK, : S - BLOCK] = g[BLOCK:, BLOCK:] - stack3(rest, rest, (0, 0))
        x[: S - BLOCK, :] = x[BLOCK:, :] - stack3(rest, split(solved), (0, 0))

    def loop(index, carry):
        beside(index)
        step(index)
        return carry

    lax.fori_loop(0, S // BLOCK - 1, loop, 0)
    before_last()
    step(S // BLOCK - 1, last=True)


def kernel(
    d_hbm, rs_hbm, w_hbm, cs_hbm, w2_hbm, ranks_hbm, out_ref,
    w_ref, w2_ref, ranks_ref,
    d_own, d_sib, d_high, d_low, w_own, w_sib, rst, rst_high, rst_low, regrouped, cs_ref,
    chunks, parts, sums, ys, ys_sib, y_high, y_low, cs_high, cs_low, w2_col,
    g, pc, projected, mixed_in, mixed_out, own_pair, xi, winv, bt_out, bt_in, bt_all, bt, first_sum,
    g_out, g_in, g_all,
    in_sem, sib_sem, gather_recv, gather_send, pass_send, pass_recv,
    z_send, z_recv, re_send, re_recv, b_send, b_recv, own_sem, g_send, g_recv, reach_sem,
):
    fiber, me = lax.axis_index("fiber"), lax.axis_index("row")
    z, core = lax.div(fiber, 2), lax.rem(fiber, 2)
    x, y = lax.div(me, SIDE), lax.rem(me, SIDE)
    other = 1 - core
    sibling = (2 * z + other, me)
    closing = []

    def at(dx, dy):
        return lax.rem(x + dx + SIDE, SIDE) * SIDE + lax.rem(y + dy + SIDE, SIDE)

    def z_peer(distance):
        return lax.rem(z + distance, CHIPS)

    def remote(src, dst, send, recv, device):
        copy = pltpu.make_async_remote_copy(
            src_ref=src, dst_ref=dst, send_sem=send, recv_sem=recv, device_id=device, device_id_type=MESH
        )
        copy.start()
        return copy

    def wait_bytes(ref, sem):
        pltpu.make_async_copy(ref, ref, sem).wait()

    def fetch(src, dst, i):
        copy = pltpu.make_async_copy(src, dst, in_sem.at[i])
        copy.start()
        return copy

    half_of_core = pl.ds(pl.multiple_of(core * HALF, HALF), HALF)
    half_of_sibling = pl.ds(pl.multiple_of(other * HALF, HALF), HALF)
    fetch_rs = fetch(rs_hbm.at[half_of_core], rst.at[me], 0)
    fetch_d = fetch(d_hbm.at[0], d_own, 1)
    fetch_cs = fetch(cs_hbm, cs_ref, 2)
    fetch_w = fetch(w_hbm, w_ref, 3)
    fetch_later = [fetch(w2_hbm, w2_ref, 4), fetch(ranks_hbm, ranks_ref, 5)]
    peers = [(fiber, at(dx, dy)) for dx, dy in OTHERS]
    peers += [(2 * z_peer(e) + core, me) for e in (1, CHIPS - 1)]
    peers += [sibling]
    barrier = pltpu.get_barrier_semaphore()
    for peer in peers:
        pl.semaphore_signal(barrier, inc=1, device_id=peer, device_id_type=MESH)
    fetch_w.wait()
    w_t = jnp.broadcast_to(w_ref[...], (LANES, S)).T
    w_own[0], w_own[1] = w_t[:HALF], w_t[HALF:]
    fetch_rs.wait()
    fetch_d.wait()
    pl.semaphore_wait(barrier, len(peers))

    def reach(step):
        if step > 0:
            pl.semaphore_wait(reach_sem.at[step - 1], 2)
        if step < 3:
            for e in (2**step, CHIPS - 2**step):
                to = (2 * z_peer(e) + core, me)
                pl.semaphore_signal(reach_sem.at[step], inc=1, device_id=to, device_id_type=MESH)

    def drain():
        while closing:
            closing.pop(0)()

    reach(0)

    def gather(buf, which):
        send = gather_send.at[which]
        closing.append(lambda: wait_bytes(rst.at[pl.ds(0, ROWS - 1)], send))

        def piece(s, slot):
            return buf(slot, s * SUB, SUB)

        def receive(s, j, d):
            if which == 1 and j > 0:
                return gather_recv.at[1, 0, 1, 0]
            return gather_recv.at[which, s, j, d - 1]

        def push(s, slot, axis, j):
            for d in (2, 1, 3):
                ref = piece(s, slot)
                to = at(d, 0) if axis == 0 else at(0, d)
                remote(ref, ref, send, receive(s, j, d), (fiber, to))

        def arrived(s, ex, ey):
            near, last = (ex, ey) if s == 0 else (ey, ex)
            sem = receive(s, 1 + near, last) if last else receive(s, 0, near)
            slot = at(-ex, -ey)
            wait_bytes(piece(s, slot), sem)
            if not last:
                push(s, slot, 1 - s, 1 + near)

        def start():
            for s in range(2):
                push(s, me, s, 0)
            for s in range(2):
                push(s, me, 1 - s, 1)

        def first():
            for e in (1, 3, 2):
                for s in range(2):
                    arrived(s, *((e, 0) if s == 0 else (0, e)))

        def rest(offsets):
            if which == 1:
                wait_bytes(rst.at[pl.ds(0, ROWS - SIDE)], receive(0, 1, 1))
                return
            for ex, ey in offsets:
                for s in range(2):
                    if (ex, ey)[1 - s]:
                        arrived(s, ex, ey)

        return start, first, rest

    def add_to(ref, first, value):
        ref[...] = value if first == 0 else ref[...] + value

    def fiber_sum(value, which, beside):
        for i in range(CHIPS):
            chunks[which, i] = value[10 * i : 10 * i + 10]
        sent, got = z_send.at[which], z_recv.at[which]
        for e in AWAY:
            to = z_peer(e)
            remote(chunks.at[which, to], parts.at[which, z], sent.at[0], got.at[0], (2 * to + core, me))
        parts[which, z] = chunks[which, z]
        beside()
        wait_bytes(parts.at[which, pl.ds(0, CHIPS - 1)], got.at[0])
        total = parts[which, 0]
        for i in range(1, CHIPS):
            total = total + parts[which, i]
        sums[which, z] = total
        for e in AWAY:
            to = z_peer(e)
            remote(sums.at[which, z], sums.at[which, z], sent.at[1], got.at[1], (2 * to + core, me))
        for i in range(2):
            closing.append(lambda i=i: wait_bytes(parts.at[which, pl.ds(0, CHIPS - 1)], sent.at[i]))
        wait_bytes(sums.at[which, pl.ds(0, CHIPS - 1)], got.at[1])
        return jnp.concatenate([sums[which, i] for i in range(CHIPS)], axis=0)

    to_sibling = [
        remote(d_own, d_sib, sib_sem.at[0, 0], sib_sem.at[1, 0], sibling),
        remote(w_own.at[other], w_sib, sib_sem.at[0, 1], sib_sem.at[1, 1], sibling),
    ]
    for copy in to_sibling:
        closing.append(copy.wait_send)

    def columns(slot):
        return pl.ds(pl.multiple_of(slot * LANES, LANES), LANES)

    def first_group(first, slots):
        if first == 0:
            fetch_cs.wait()
            for copy in fetch_later:
                copy.wait()
            cs_high[...], cs_low[...] = split(cs_ref[...].T)
            w2_col[...] = jnp.broadcast_to(w2_ref[...], (LANES, S)).T
            for copy in to_sibling:
                copy.wait_recv()
            i = 0
            for offsets in GROUPS:
                for ex, ey in offsets:
                    cols = columns(at(-ex, -ey))
                    here = slice(i * LANES, (i + 1) * LANES)
                    d_high[:LANES, here], d_low[:LANES, here] = split(d_own[:, cols])
                    d_high[LANES:, here], d_low[LANES:, here] = split(d_sib[:, cols])
                    i += 1
        for i, slot in enumerate(slots):
            here = slice((first + i) * LANES, (first + i + 1) * LANES)
            rst_high[:, here], rst_low[:, here] = split(rst[slot])
        here = slice(first * LANES, (first + len(slots)) * LANES)
        add_to(
            first_sum, first, dot3((rst_high[:, here], rst_low[:, here]), (d_high[:, here], d_low[:, here]), (1, 1))
        )

    start, first, rest = gather(lambda slot, start, size: rst.at[slot, pl.ds(start, size)], 0)
    start()
    reach(1)
    first()
    reach(2)
    count = 0
    for offsets in GROUPS:
        rest(offsets)
        first_group(count, [at(-ex, -ey) for ex, ey in offsets])
        count += len(offsets)
    def regroup():
        for dx, dy in OTHERS:
            to = at(dx, dy)
            remote(d_own.at[:, columns(to)], regrouped.at[me], re_send, re_recv, (fiber, to))
        regrouped[me] = d_own[:, columns(me)]

    reach(3)
    one = fiber_sum(first_sum[:, :LANES] * w_own[core] + first_sum[:, LANES:] * w_sib[...], 0, regroup)
    closing.append(lambda: wait_bytes(regrouped.at[pl.ds(0, ROWS - 1)], re_send))

    def to_pair(value, which):
        own_pair[which, core] = value
        ref = own_pair.at[which, core]
        copy = remote(ref, ref, own_sem.at[0, which], own_sem.at[1, which], sibling)
        closing.append(copy.wait_send)
        copy.wait_recv()
        return own_pair[which].reshape(S, LANES)

    def gram_sum(block, which, beside):
        high, low = split(jnp.concatenate([block, jnp.zeros((LANES // 2, LANES), F32)], axis=0))
        for c, first in ((0, 0), (1, LANES)):

            @pl.when(core == c)
            def _():
                last = LANES if c == 0 else 3 * LANES
                part = stack3((high[first:last], low[first:last]), (high[first:], low[first:]), (1, 1))
                for i in range(ROWS):
                    strip = part[8 * i : 8 * i + 8]
                    if c == 0:
                        tiles = [strip[:, LANES * t : LANES * (t + 1)] for t in range(3)]
                    else:
                        tiles = [strip[:, :LANES], strip[:, LANES:], part[LANES + 8 * i : LANES + 8 * i + 8, LANES:]]
                    for t in range(3):
                        g_out[which, i, t] = tiles[t]

        for dx, dy in OTHERS:
            to = at(dx, dy)
            remote(g_out.at[which, to], g_in.at[which, me], g_send.at[which, 0], g_recv.at[which, 0], (fiber, to))
        g_in[which, me] = g_out[which, me]
        beside[0]()
        wait_bytes(g_in.at[which, pl.ds(0, ROWS - 1)], g_recv.at[which, 0])
        total = g_in[which, 0]
        for i in range(1, ROWS):
            total = total + g_in[which, i]
        g_all[which, core, me] = total
        ref = g_all.at[which, core, me]
        for dx, dy in OTHERS:
            to = at(dx, dy)
            remote(ref, ref, g_send.at[which, 1], g_recv.at[which, 1], (fiber, to))
            remote(ref, ref, g_send.at[which, 2], g_recv.at[which, 2], (2 * z + other, to))
        remote(ref, ref, g_send.at[which, 2], g_recv.at[which, 2], sibling)
        for i in range(2):
            closing.append(lambda i=i: wait_bytes(g_in.at[which, pl.ds(0, ROWS - 1)], g_send.at[which, i]))
        closing.append(lambda: wait_bytes(g_in.at[which], g_send.at[which, 2]))
        beside[1]()
        wait_bytes(g_all.at[which, core, pl.ds(0, ROWS - 1)], g_recv.at[which, 1])
        wait_bytes(g_all.at[which, other], g_recv.at[which, 2])
        for i in range(ROWS):
            strip, under = slice(8 * i, 8 * i + 8), slice(LANES + 8 * i, LANES + 8 * i + 8)
            g[strip, :LANES] = g_all[which, 0, i, 0]
            g[strip, LANES : 2 * LANES] = g_all[which, 0, i, 1]
            g[strip, 2 * LANES :] = g_all[which, 0, i, 2][:, : LANES // 2]
            g[under, LANES : 2 * LANES] = g_all[which, 1, i, 0]
            g[under, 2 * LANES :] = g_all[which, 1, i, 1][:, : LANES // 2]
            if i < ROWS // 2:
                g[2 * LANES + 8 * i : 2 * LANES + 8 * i + 8, 2 * LANES :] = g_all[which, 1, i, 2][:, : LANES // 2]

    square = (S, S)
    identity = jnp.where(
        lax.broadcasted_iota(jnp.int32, square, 0) == lax.broadcasted_iota(jnp.int32, square, 1), 1.0, 0.0
    )
    g[...] = identity
    xi[0], xi[1] = identity, identity
    block_one = to_pair(one, 0)
    ys[me] = one
    start, first, rest = gather(lambda slot, start, size: ys.at[slot, pl.ds(start, size)], 1)
    gram_sum(block_one, 0, (start, first))

    def pass_on(index):
        @pl.when(index == 1)
        def _():
            rest(None)
            remote(ys, ys_sib, pass_send, pass_recv, sibling)

    def project_one():
        wait_bytes(ys_sib, pass_recv)
        wait_bytes(regrouped.at[pl.ds(0, ROWS - 1)], re_recv)
        for j in range(ROWS):
            here = slice(j * LANES, (j + 1) * LANES)
            y_high[half_of_core, here], y_low[half_of_core, here] = split(ys[j])
            y_high[half_of_sibling, here], y_low[half_of_sibling, here] = split(ys_sib[j])
        slabs = split(regrouped[...].reshape(ROWS * LANES, LANES))
        projected[...] = dot3((y_high[...], y_low[...]), slabs, (1, 0))

    cholesky_inverse(g, xi.at[0], winv, pass_on, project_one)
    closing.append(lambda: wait_bytes(ys, pass_send))
    index = lax.broadcasted_iota(jnp.int32, (S, LANES), 0)
    pc[...] = jnp.where(index < ranks_ref[0], dot3(split(winv[...]), split(projected[...]), (1, 0)), 0.0)

    pc_pair = split(pc[...])
    mixed = dot3((cs_high[...], cs_low[...]), pc_pair, (1, 0)) * w2_col[...]
    mixed_out[0], mixed_out[1] = mixed[:HALF], mixed[HALF:]
    exchange = remote(mixed_out.at[other], mixed_in, sib_sem.at[0, 2], sib_sem.at[1, 2], sibling)
    closing.append(exchange.wait_send)
    exchange.wait_recv()
    block_two = to_pair(fiber_sum(mixed_out[core] + mixed_in[...], 1, drain), 1)

    def nothing():
        pass

    def project_two():
        drain()
        bt_part = dot3(split(block_two), pc_pair, (1, 1))
        for j in range(ROWS):
            bt_out[j] = bt_part[20 * j : 20 * j + 20]

    gram_sum(block_two, 1, (nothing, project_two))
    for dx, dy in OTHERS:
        to = at(dx, dy)
        remote(bt_out.at[to], bt_in.at[me], b_send.at[0], b_recv.at[0], (fiber, to))
    bt_in[me] = bt_out[me]

    def add_up(index):
        @pl.when(index == 2)
        def _():
            wait_bytes(bt_in.at[pl.ds(0, ROWS - 1)], b_recv.at[0])
            total = bt_in[0]
            for j in range(1, ROWS):
                total = total + bt_in[j]
            bt_all[me] = total
            for dx, dy in OTHERS:
                to = at(dx, dy)
                remote(bt_all.at[me], bt_all.at[me], b_send.at[1], b_recv.at[1], (fiber, to))

    def assemble():
        wait_bytes(bt_all.at[pl.ds(0, ROWS - 1)], b_recv.at[1])
        for j in range(ROWS):
            bt[20 * j : 20 * j + 20, :] = bt_all[j]

    cholesky_inverse(g, xi.at[1], winv, add_up, assemble)
    odd = lax.rem(me, 2)
    window = winv[pl.ds(pl.multiple_of(20 * me - 4 * odd, 8), 24), :]
    mine = jnp.where(odd == 0, window[:20], window[4:])
    keep = lax.broadcasted_iota(jnp.int32, mine.shape, 0) + 20 * me < ranks_ref[1]
    mine = jnp.where(keep, mine, 0.0)
    core_t = dot3(split(mine), split(bt[...]), (1, 0))
    for i in range(S // ROWS):
        out_ref[i] = core_t[i : i + 1]
    drain()
    for i in range(2):
        wait_bytes(bt_all.at[pl.ds(0, ROWS - 1)], b_send.at[i])


def local(deltas, row_sketch, slab_sketch, core_sketch, slab_sketch_two, ranks):
    vmem = lambda *shape: pltpu.VMEM(shape, F32)
    half = lambda *shape: pltpu.VMEM(shape, BF16)
    dma = pltpu.SemaphoreType.DMA
    in_hbm = pl.BlockSpec(memory_space=pltpu.HBM)
    core_t = pl.pallas_call(
        kernel,
        out_shape=jax.ShapeDtypeStruct((S // ROWS, 1, S), F32),
        in_specs=[in_hbm] * 6,
        out_specs=pl.BlockSpec(memory_space=pltpu.VMEM),
        scratch_shapes=[
            vmem(1, S), vmem(1, S), pltpu.SMEM((2,), jnp.int32),
            vmem(LANES, 2048), vmem(LANES, 2048),
            half(2 * LANES, 2048), half(2 * LANES, 2048),
            vmem(2, HALF, LANES), vmem(HALF, LANES),
            vmem(ROWS, HALF, LANES), half(HALF, 2048), half(HALF, 2048),
            vmem(ROWS, LANES, LANES), vmem(S, S),
            vmem(2, CHIPS, 10, LANES), vmem(2, CHIPS, 10, LANES), vmem(2, CHIPS, 10, LANES),
            vmem(ROWS, HALF, LANES), vmem(ROWS, HALF, LANES),
            half(S, 2048), half(S, 2048),
            half(S, S), half(S, S), vmem(S, LANES),
            vmem(S, S), vmem(S, LANES), vmem(S, LANES),
            vmem(HALF, LANES), vmem(2, HALF, LANES), vmem(2, 2, HALF, LANES),
            vmem(2, S, S), vmem(S, S),
            vmem(ROWS, 20, S), vmem(ROWS, 20, S), vmem(ROWS, 20, S), vmem(S, S),
            vmem(HALF, 2 * LANES),
            vmem(2, ROWS, 3, 8, LANES), vmem(2, ROWS, 3, 8, LANES), vmem(2, 2, ROWS, 3, 8, LANES),
            dma((6,)), dma((2, 3)),
            dma((2, 2, 5, 3)), dma((2,)),
            dma(()), dma(()),
            dma((2, 2)), dma((2, 2)),
            dma(()), dma(()),
            dma((2,)), dma((2,)),
            dma((2, 2)), dma((2, 3)), dma((2, 3)),
            pltpu.SemaphoreType.REGULAR((3,)),
        ],
        compiler_params=pltpu.CompilerParams(
            collective_id=0, has_side_effects=True, vmem_limit_bytes=62 * 2**20
        ),
        cost_estimate=pl.CostEstimate(flops=2 * 10**9, bytes_accessed=4 * 10**6, transcendentals=0),
    )(deltas, row_sketch.T, slab_sketch, core_sketch, slab_sketch_two, ranks)
    return jnp.transpose(core_t, (1, 2, 0))


def solution(mesh):
    in_specs = (
        P("fiber", "row", None),
        P("row", None),
        P("fiber", None),
        P(),
        P("fiber", None),
        P(),
    )
    out_specs = P("fiber", None, "row")
    return jax.shard_map(local, mesh=mesh, in_specs=in_specs, out_specs=out_specs, check_vma=False)
```

```python
import jax
import jax.numpy as jnp
from jax import lax
from jax.experimental import pallas as pl
from jax.experimental.pallas import tpu as pltpu
from jax.sharding import PartitionSpec as P

F32, BF16 = jnp.float32, jnp.bfloat16
MESH = pl.DeviceIdType.MESH
S, HALF, SUB, BLOCK = 320, 160, 80, 64
SIDE = 4
ROWS = SIDE * SIDE
CHIPS = 16
LANES = 128
CROSS = [(0, 0), (1, 0), (3, 0), (0, 1), (0, 3), (2, 0), (0, 2)]
DIAGONAL = [(1, 1), (1, 3), (3, 1), (3, 3)]
FAR = [(1, 2), (3, 2), (2, 1), (2, 3), (2, 2)]
GROUPS = [CROSS, DIAGONAL, FAR]
OTHERS = [offset for group in GROUPS[::-1] for offset in group[::-1] if offset != (0, 0)]
AWAY = [8, 7, 9, 6, 10, 5, 11, 4, 12, 3, 13, 2, 14, 1, 15]


def split(value):
    high = value.astype(BF16)
    return high, (value - high.astype(F32)).astype(BF16)


def dot3(left, right, contract):
    numbers = ((contract[:1], contract[1:]), ((), ()))

    def one(a, b):
        return lax.dot_general(a, b, numbers, preferred_element_type=F32)

    (ah, al), (bh, bl) = left, right
    return one(ah, bh) + (one(ah, bl) + one(al, bh))


def stack3(left, right, contract):
    (ah, al), (bh, bl) = left, right
    return lax.dot_general(
        jnp.concatenate([ah, ah, al], axis=contract[0]),
        jnp.concatenate([bh, bl, bh], axis=contract[1]),
        (((contract[0],), (contract[1],)), ((), ())),
        preferred_element_type=F32,
    )


def factor_block(rows):
    sub = lax.broadcasted_iota(jnp.int32, (8, LANES), 0)

    def wide(piece):
        return jnp.broadcast_to(piece, (8, LANES))

    def lane_of(array, lane):
        return jnp.take_along_axis(array, jnp.full((8, LANES), lane, jnp.int32), axis=1)

    rows, outs = list(rows), []
    for p in range(8):
        row = [wide(rows[p][k : k + 1, :]) for k in range(8)]
        own = [lane_of(rows[p], 8 * p + k) for k in range(8)]
        a = {(i, k): wide(own[k][i : i + 1, :]) for k in range(8) for i in range(k, 8)}
        col = [lane_of(rows[p + 1], 8 * p + k) for k in range(8)] if p < 7 else None
        out = None
        for k in range(8):
            inverse = 1.0 / a[k, k]
            for j in range(k + 1, 8):
                factor = a[j, k] * inverse
                for i in range(j, 8):
                    a[i, j] = a[i, j] - a[i, k] * factor
                row[j] = row[j] - factor * row[k]
                if col:
                    col[j] = col[j] - factor * col[k]
            if col:
                rows[p + 1] = rows[p + 1] - col[k] * (row[k] * inverse)
            final = row[k] * lax.rsqrt(a[k, k])
            out = final if out is None else jnp.where(sub == k, final, out)
        outs.append(out)
        if p < 6:
            high = out.astype(BF16).astype(F32)
            low = out - high
            left = jnp.concatenate([high, high, low], axis=0)[:, :BLOCK].astype(BF16)
            right = jnp.concatenate([high, low, high], axis=0).astype(BF16)
            update = lax.dot_general(left, right, (((0,), (0,)), ((), ())), preferred_element_type=F32)
            for i in range(p + 2, 8):
                rows[i] = rows[i] - update[8 * i : 8 * i + 8]
    return outs


def cholesky_inverse(g, x, done, beside, before_last):
    lane = lax.broadcasted_iota(jnp.int32, (8, LANES), 1)
    sub = lax.broadcasted_iota(jnp.int32, (8, LANES), 0)

    def step(index, last=False):
        rows = [
            jnp.where(
                lane < BLOCK,
                g[8 * i : 8 * i + 8, :LANES],
                jnp.where(lane - BLOCK == sub + 8 * i, 1.0, 0.0),
            )
            for i in range(8)
        ]
        block = jnp.concatenate(factor_block(rows), axis=0)
        inverse = split(block[:, BLOCK:])
        solved = stack3(inverse, split(x[:BLOCK, :]), (1, 0))
        if last:
            done[S - BLOCK :, :] = solved
            return
        done[pl.ds(pl.multiple_of(index * BLOCK, BLOCK), BLOCK), :] = solved
        upper = stack3(inverse, split(g[:BLOCK, :]), (1, 0))
        rest = split(upper[:, BLOCK:])
        g[: S - BLOCK, : S - BLOCK] = g[BLOCK:, BLOCK:] - stack3(rest, rest, (0, 0))
        x[: S - BLOCK, :] = x[BLOCK:, :] - stack3(rest, split(solved), (0, 0))

    def loop(index, carry):
        beside(index)
        step(index)
        return carry

    lax.fori_loop(0, S // BLOCK - 1, loop, 0)
    before_last()
    step(S // BLOCK - 1, last=True)


def kernel(
    d_hbm, rs_hbm, w_hbm, cs_hbm, w2_hbm, ranks_hbm, out_ref,
    w_ref, w2_ref, ranks_ref,
    d_own, d_sib, d_high, d_low, w_own, w_sib, rst, rst_high, rst_low, regrouped, cs_ref,
    chunks, parts, sums, ys, ys_sib, y_high, y_low, cs_high, cs_low, w2_col,
    g, pc, projected, mixed_in, mixed_out, own_pair, xi, winv, bt_out, bt_in, bt_all, bt, first_sum,
    g_out, g_in, g_all,
    in_sem, sib_sem, gather_recv, gather_send, pass_send, pass_recv,
    z_send, z_recv, re_send, re_recv, b_send, b_recv, own_sem, g_send, g_recv, reach_sem,
):
    fiber, me = lax.axis_index("fiber"), lax.axis_index("row")
    z, core = lax.div(fiber, 2), lax.rem(fiber, 2)
    x, y = lax.div(me, SIDE), lax.rem(me, SIDE)
    other = 1 - core
    sibling = (2 * z + other, me)
    closing = []

    def at(dx, dy):
        return lax.rem(x + dx + SIDE, SIDE) * SIDE + lax.rem(y + dy + SIDE, SIDE)

    def z_peer(distance):
        return lax.rem(z + distance, CHIPS)

    def remote(src, dst, send, recv, device):
        copy = pltpu.make_async_remote_copy(
            src_ref=src, dst_ref=dst, send_sem=send, recv_sem=recv, device_id=device, device_id_type=MESH
        )
        copy.start()
        return copy

    def wait_bytes(ref, sem):
        pltpu.make_async_copy(ref, ref, sem).wait()

    def fetch(src, dst, i):
        copy = pltpu.make_async_copy(src, dst, in_sem.at[i])
        copy.start()
        return copy

    half_of_core = pl.ds(pl.multiple_of(core * HALF, HALF), HALF)
    half_of_sibling = pl.ds(pl.multiple_of(other * HALF, HALF), HALF)
    fetch_rs = fetch(rs_hbm.at[half_of_core], rst.at[me], 0)
    fetch_d = fetch(d_hbm.at[0], d_own, 1)
    fetch_cs = fetch(cs_hbm, cs_ref, 2)
    fetch_w = fetch(w_hbm, w_ref, 3)
    fetch_later = [fetch(w2_hbm, w2_ref, 4), fetch(ranks_hbm, ranks_ref, 5)]
    peers = [(fiber, at(dx, dy)) for dx, dy in OTHERS]
    peers += [(2 * z_peer(e) + core, me) for e in (1, CHIPS - 1)]
    peers += [sibling]
    barrier = pltpu.get_barrier_semaphore()
    for peer in peers:
        pl.semaphore_signal(barrier, inc=1, device_id=peer, device_id_type=MESH)
    fetch_w.wait()
    w_t = jnp.broadcast_to(w_ref[...], (LANES, S)).T
    w_own[0], w_own[1] = w_t[:HALF], w_t[HALF:]
    fetch_rs.wait()
    fetch_d.wait()
    pl.semaphore_wait(barrier, len(peers))

    def reach(step):
        if step > 0:
            pl.semaphore_wait(reach_sem.at[step - 1], 2)
        if step < 3:
            for e in (2**step, CHIPS - 2**step):
                to = (2 * z_peer(e) + core, me)
                pl.semaphore_signal(reach_sem.at[step], inc=1, device_id=to, device_id_type=MESH)

    def drain():
        while closing:
            closing.pop(0)()

    reach(0)

    def gather(buf, which):
        send = gather_send.at[which]
        closing.append(lambda: wait_bytes(rst.at[pl.ds(0, ROWS - 1)], send))

        def piece(s, slot):
            return buf(slot, s * SUB, SUB)

        def receive(s, j, d):
            if which == 1 and j > 0:
                return gather_recv.at[1, 0, 1, 0]
            return gather_recv.at[which, s, j, d - 1]

        def push(s, slot, axis, j):
            for d in (2, 1, 3):
                ref = piece(s, slot)
                to = at(d, 0) if axis == 0 else at(0, d)
                remote(ref, ref, send, receive(s, j, d), (fiber, to))

        def arrived(s, ex, ey):
            near, last = (ex, ey) if s == 0 else (ey, ex)
            sem = receive(s, 1 + near, last) if last else receive(s, 0, near)
            slot = at(-ex, -ey)
            wait_bytes(piece(s, slot), sem)
            if not last:
                push(s, slot, 1 - s, 1 + near)

        def start():
            for s in range(2):
                push(s, me, s, 0)
            for s in range(2):
                push(s, me, 1 - s, 1)

        def first():
            for e in (1, 3, 2):
                for s in range(2):
                    arrived(s, *((e, 0) if s == 0 else (0, e)))

        def rest(offsets):
            if which == 1:
                wait_bytes(rst.at[pl.ds(0, ROWS - SIDE)], receive(0, 1, 1))
                return
            for ex, ey in offsets:
                for s in range(2):
                    if (ex, ey)[1 - s]:
                        arrived(s, ex, ey)

        return start, first, rest

    def add_to(ref, first, value):
        ref[...] = value if first == 0 else ref[...] + value

    def fiber_sum(value, which, beside):
        for i in range(CHIPS):
            chunks[which, i] = value[10 * i : 10 * i + 10]
        sent, got = z_send.at[which], z_recv.at[which]
        for e in AWAY:
            to = z_peer(e)
            remote(chunks.at[which, to], parts.at[which, z], sent.at[0], got.at[0], (2 * to + core, me))
        parts[which, z] = chunks[which, z]
        beside()
        wait_bytes(parts.at[which, pl.ds(0, CHIPS - 1)], got.at[0])
        total = parts[which, 0]
        for i in range(1, CHIPS):
            total = total + parts[which, i]
        sums[which, z] = total
        for e in AWAY:
            to = z_peer(e)
            remote(sums.at[which, z], sums.at[which, z], sent.at[1], got.at[1], (2 * to + core, me))
        for i in range(2):
            closing.append(lambda i=i: wait_bytes(parts.at[which, pl.ds(0, CHIPS - 1)], sent.at[i]))
        wait_bytes(sums.at[which, pl.ds(0, CHIPS - 1)], got.at[1])
        return jnp.concatenate([sums[which, i] for i in range(CHIPS)], axis=0)

    to_sibling = [
        remote(d_own, d_sib, sib_sem.at[0, 0], sib_sem.at[1, 0], sibling),
        remote(w_own.at[other], w_sib, sib_sem.at[0, 1], sib_sem.at[1, 1], sibling),
    ]
    for copy in to_sibling:
        closing.append(copy.wait_send)

    def columns(slot):
        return pl.ds(pl.multiple_of(slot * LANES, LANES), LANES)

    def first_group(first, slots):
        if first == 0:
            fetch_cs.wait()
            for copy in fetch_later:
                copy.wait()
            cs_high[...], cs_low[...] = split(cs_ref[...].T)
            w2_col[...] = jnp.broadcast_to(w2_ref[...], (LANES, S)).T
            for copy in to_sibling:
                copy.wait_recv()
            i = 0
            for offsets in GROUPS:
                for ex, ey in offsets:
                    cols = columns(at(-ex, -ey))
                    here = slice(i * LANES, (i + 1) * LANES)
                    d_high[:LANES, here], d_low[:LANES, here] = split(d_own[:, cols])
                    d_high[LANES:, here], d_low[LANES:, here] = split(d_sib[:, cols])
                    i += 1
        for i, slot in enumerate(slots):
            here = slice((first + i) * LANES, (first + i + 1) * LANES)
            rst_high[:, here], rst_low[:, here] = split(rst[slot])
        here = slice(first * LANES, (first + len(slots)) * LANES)
        add_to(
            first_sum, first, dot3((rst_high[:, here], rst_low[:, here]), (d_high[:, here], d_low[:, here]), (1, 1))
        )

    start, first, rest = gather(lambda slot, start, size: rst.at[slot, pl.ds(start, size)], 0)
    start()
    reach(1)
    first()
    reach(2)
    count = 0
    for offsets in GROUPS:
        rest(offsets)
        first_group(count, [at(-ex, -ey) for ex, ey in offsets])
        count += len(offsets)
    def regroup():
        for dx, dy in OTHERS:
            to = at(dx, dy)
            remote(d_own.at[:, columns(to)], regrouped.at[me], re_send, re_recv, (fiber, to))
        regrouped[me] = d_own[:, columns(me)]
        square = (S, S)
        identity = jnp.where(
            lax.broadcasted_iota(jnp.int32, square, 0) == lax.broadcasted_iota(jnp.int32, square, 1), 1.0, 0.0
        )
        g[...] = identity
        xi[0], xi[1] = identity, identity

    reach(3)
    one = fiber_sum(first_sum[:, :LANES] * w_own[core] + first_sum[:, LANES:] * w_sib[...], 0, regroup)
    closing.append(lambda: wait_bytes(regrouped.at[pl.ds(0, ROWS - 1)], re_send))

    def to_pair(value, which):
        own_pair[which, core] = value
        ref = own_pair.at[which, core]
        copy = remote(ref, ref, own_sem.at[0, which], own_sem.at[1, which], sibling)
        closing.append(copy.wait_send)
        copy.wait_recv()
        return own_pair[which].reshape(S, LANES)

    def gram_sum(block, which, beside):
        high, low = split(jnp.concatenate([block, jnp.zeros((LANES // 2, LANES), F32)], axis=0))
        for c, first in ((0, 0), (1, LANES)):

            @pl.when(core == c)
            def _():
                last = LANES if c == 0 else 3 * LANES
                part = stack3((high[first:last], low[first:last]), (high[first:], low[first:]), (1, 1))
                for i in range(ROWS):
                    strip = part[8 * i : 8 * i + 8]
                    if c == 0:
                        tiles = [strip[:, LANES * t : LANES * (t + 1)] for t in range(3)]
                    else:
                        tiles = [strip[:, :LANES], strip[:, LANES:], part[LANES + 8 * i : LANES + 8 * i + 8, LANES:]]
                    for t in range(3):
                        g_out[which, i, t] = tiles[t]

        for dx, dy in OTHERS:
            to = at(dx, dy)
            remote(g_out.at[which, to], g_in.at[which, me], g_send.at[which, 0], g_recv.at[which, 0], (fiber, to))
        g_in[which, me] = g_out[which, me]
        beside[0]()
        wait_bytes(g_in.at[which, pl.ds(0, ROWS - 1)], g_recv.at[which, 0])
        total = g_in[which, 0]
        for i in range(1, ROWS):
            total = total + g_in[which, i]
        g_all[which, core, me] = total
        ref = g_all.at[which, core, me]
        for dx, dy in OTHERS:
            to = at(dx, dy)
            remote(ref, ref, g_send.at[which, 1], g_recv.at[which, 1], (fiber, to))
            remote(ref, ref, g_send.at[which, 2], g_recv.at[which, 2], (2 * z + other, to))
        remote(ref, ref, g_send.at[which, 2], g_recv.at[which, 2], sibling)
        for i in range(2):
            closing.append(lambda i=i: wait_bytes(g_in.at[which, pl.ds(0, ROWS - 1)], g_send.at[which, i]))
        closing.append(lambda: wait_bytes(g_in.at[which], g_send.at[which, 2]))
        beside[1]()
        wait_bytes(g_all.at[which, core, pl.ds(0, ROWS - 1)], g_recv.at[which, 1])
        wait_bytes(g_all.at[which, other], g_recv.at[which, 2])
        for i in range(ROWS):
            strip, under = slice(8 * i, 8 * i + 8), slice(LANES + 8 * i, LANES + 8 * i + 8)
            g[strip, :LANES] = g_all[which, 0, i, 0]
            g[strip, LANES : 2 * LANES] = g_all[which, 0, i, 1]
            g[strip, 2 * LANES :] = g_all[which, 0, i, 2][:, : LANES // 2]
            g[under, LANES : 2 * LANES] = g_all[which, 1, i, 0]
            g[under, 2 * LANES :] = g_all[which, 1, i, 1][:, : LANES // 2]
            if i < ROWS // 2:
                g[2 * LANES + 8 * i : 2 * LANES + 8 * i + 8, 2 * LANES :] = g_all[which, 1, i, 2][:, : LANES // 2]

    block_one = to_pair(one, 0)
    ys[me] = one
    start, first, rest = gather(lambda slot, start, size: ys.at[slot, pl.ds(start, size)], 1)
    gram_sum(block_one, 0, (start, first))

    def pass_on(index):
        @pl.when(index == 1)
        def _():
            rest(None)
            remote(ys, ys_sib, pass_send, pass_recv, sibling)

    def project_one():
        wait_bytes(ys_sib, pass_recv)
        wait_bytes(regrouped.at[pl.ds(0, ROWS - 1)], re_recv)
        for j in range(ROWS):
            here = slice(j * LANES, (j + 1) * LANES)
            y_high[half_of_core, here], y_low[half_of_core, here] = split(ys[j])
            y_high[half_of_sibling, here], y_low[half_of_sibling, here] = split(ys_sib[j])
        slabs = split(regrouped[...].reshape(ROWS * LANES, LANES))
        projected[...] = dot3((y_high[...], y_low[...]), slabs, (1, 0))

    cholesky_inverse(g, xi.at[0], winv, pass_on, project_one)
    closing.append(lambda: wait_bytes(ys, pass_send))
    index = lax.broadcasted_iota(jnp.int32, (S, LANES), 0)
    pc[...] = jnp.where(index < ranks_ref[0], dot3(split(winv[...]), split(projected[...]), (1, 0)), 0.0)

    pc_pair = split(pc[...])
    mixed = dot3((cs_high[...], cs_low[...]), pc_pair, (1, 0)) * w2_col[...]
    mixed_out[0], mixed_out[1] = mixed[:HALF], mixed[HALF:]
    exchange = remote(mixed_out.at[other], mixed_in, sib_sem.at[0, 2], sib_sem.at[1, 2], sibling)
    closing.append(exchange.wait_send)
    exchange.wait_recv()
    block_two = to_pair(fiber_sum(mixed_out[core] + mixed_in[...], 1, drain), 1)

    def nothing():
        pass

    def project_two():
        drain()
        bt_part = dot3(split(block_two), pc_pair, (1, 1))
        for j in range(ROWS):
            bt_out[j] = bt_part[20 * j : 20 * j + 20]
        for dx, dy in OTHERS:
            to = at(dx, dy)
            remote(bt_out.at[to], bt_in.at[me], b_send.at[0], b_recv.at[0], (fiber, to))
        bt_in[me] = bt_out[me]


    gram_sum(block_two, 1, (nothing, project_two))
    def add_up(index):
        @pl.when(index == 2)
        def _():
            wait_bytes(bt_in.at[pl.ds(0, ROWS - 1)], b_recv.at[0])
            total = bt_in[0]
            for j in range(1, ROWS):
                total = total + bt_in[j]
            bt_all[me] = total
            for dx, dy in OTHERS:
                to = at(dx, dy)
                remote(bt_all.at[me], bt_all.at[me], b_send.at[1], b_recv.at[1], (fiber, to))

    def assemble():
        wait_bytes(bt_all.at[pl.ds(0, ROWS - 1)], b_recv.at[1])
        for j in range(ROWS):
            bt[20 * j : 20 * j + 20, :] = bt_all[j]

    cholesky_inverse(g, xi.at[1], winv, add_up, assemble)
    odd = lax.rem(me, 2)
    window = winv[pl.ds(pl.multiple_of(20 * me - 4 * odd, 8), 24), :]
    mine = jnp.where(odd == 0, window[:20], window[4:])
    keep = lax.broadcasted_iota(jnp.int32, mine.shape, 0) + 20 * me < ranks_ref[1]
    mine = jnp.where(keep, mine, 0.0)
    core_t = dot3(split(mine), split(bt[...]), (1, 0))
    for i in range(S // ROWS):
        out_ref[i] = core_t[i : i + 1]
    drain()
    for i in range(2):
        wait_bytes(bt_all.at[pl.ds(0, ROWS - 1)], b_send.at[i])


def local(deltas, row_sketch, slab_sketch, core_sketch, slab_sketch_two, ranks):
    vmem = lambda *shape: pltpu.VMEM(shape, F32)
    half = lambda *shape: pltpu.VMEM(shape, BF16)
    dma = pltpu.SemaphoreType.DMA
    in_hbm = pl.BlockSpec(memory_space=pltpu.HBM)
    core_t = pl.pallas_call(
        kernel,
        out_shape=jax.ShapeDtypeStruct((S // ROWS, 1, S), F32),
        in_specs=[in_hbm] * 6,
        out_specs=pl.BlockSpec(memory_space=pltpu.VMEM),
        scratch_shapes=[
            vmem(1, S), vmem(1, S), pltpu.SMEM((2,), jnp.int32),
            vmem(LANES, 2048), vmem(LANES, 2048),
            half(2 * LANES, 2048), half(2 * LANES, 2048),
            vmem(2, HALF, LANES), vmem(HALF, LANES),
            vmem(ROWS, HALF, LANES), half(HALF, 2048), half(HALF, 2048),
            vmem(ROWS, LANES, LANES), vmem(S, S),
            vmem(2, CHIPS, 10, LANES), vmem(2, CHIPS, 10, LANES), vmem(2, CHIPS, 10, LANES),
            vmem(ROWS, HALF, LANES), vmem(ROWS, HALF, LANES),
            half(S, 2048), half(S, 2048),
            half(S, S), half(S, S), vmem(S, LANES),
            vmem(S, S), vmem(S, LANES), vmem(S, LANES),
            vmem(HALF, LANES), vmem(2, HALF, LANES), vmem(2, 2, HALF, LANES),
            vmem(2, S, S), vmem(S, S),
            vmem(ROWS, 20, S), vmem(ROWS, 20, S), vmem(ROWS, 20, S), vmem(S, S),
            vmem(HALF, 2 * LANES),
            vmem(2, ROWS, 3, 8, LANES), vmem(2, ROWS, 3, 8, LANES), vmem(2, 2, ROWS, 3, 8, LANES),
            dma((6,)), dma((2, 3)),
            dma((2, 2, 5, 3)), dma((2,)),
            dma(()), dma(()),
            dma((2, 2)), dma((2, 2)),
            dma(()), dma(()),
            dma((2,)), dma((2,)),
            dma((2, 2)), dma((2, 3)), dma((2, 3)),
            pltpu.SemaphoreType.REGULAR((3,)),
        ],
        compiler_params=pltpu.CompilerParams(
            collective_id=0, has_side_effects=True, vmem_limit_bytes=62 * 2**20
        ),
        cost_estimate=pl.CostEstimate(flops=2 * 10**9, bytes_accessed=4 * 10**6, transcendentals=0),
    )(deltas, row_sketch.T, slab_sketch, core_sketch, slab_sketch_two, ranks)
    return jnp.transpose(core_t, (1, 2, 0))


def solution(mesh):
    in_specs = (
        P("fiber", "row", None),
        P("row", None),
        P("fiber", None),
        P(),
        P("fiber", None),
        P(),
    )
    out_specs = P("fiber", None, "row")
    return jax.shard_map(local, mesh=mesh, in_specs=in_specs, out_specs=out_specs, check_vma=False)
```

```python
import jax
import jax.numpy as jnp
from jax import lax
from jax.experimental import pallas as pl
from jax.experimental.pallas import tpu as pltpu
from jax.sharding import PartitionSpec as P

F32, BF16 = jnp.float32, jnp.bfloat16
MESH = pl.DeviceIdType.MESH
S, HALF, SUB, BLOCK = 320, 160, 80, 64
SIDE = 4
ROWS = SIDE * SIDE
CHIPS = 16
LANES = 128
CROSS = [(0, 0), (1, 0), (3, 0), (0, 1), (0, 3), (2, 0), (0, 2)]
DIAGONAL = [(1, 1), (1, 3), (3, 1), (3, 3)]
FAR = [(1, 2), (3, 2), (2, 1), (2, 3), (2, 2)]
GROUPS = [CROSS, DIAGONAL, FAR]
OTHERS = [offset for group in GROUPS[::-1] for offset in group[::-1] if offset != (0, 0)]
AWAY = [8, 7, 9, 6, 10, 5, 11, 4, 12, 3, 13, 2, 14, 1, 15]


def split(value):
    high = value.astype(BF16)
    return high, (value - high.astype(F32)).astype(BF16)


def dot3(left, right, contract):
    numbers = ((contract[:1], contract[1:]), ((), ()))

    def one(a, b):
        return lax.dot_general(a, b, numbers, preferred_element_type=F32)

    (ah, al), (bh, bl) = left, right
    return one(ah, bh) + (one(ah, bl) + one(al, bh))


def stack3(left, right, contract):
    (ah, al), (bh, bl) = left, right
    return lax.dot_general(
        jnp.concatenate([ah, ah, al], axis=contract[0]),
        jnp.concatenate([bh, bl, bh], axis=contract[1]),
        (((contract[0],), (contract[1],)), ((), ())),
        preferred_element_type=F32,
    )


def factor_block(rows):
    sub = lax.broadcasted_iota(jnp.int32, (8, LANES), 0)

    def wide(piece):
        return jnp.broadcast_to(piece, (8, LANES))

    def lane_of(array, lane):
        return jnp.take_along_axis(array, jnp.full((8, LANES), lane, jnp.int32), axis=1)

    rows, outs = list(rows), []
    for p in range(8):
        row = [wide(rows[p][k : k + 1, :]) for k in range(8)]
        own = [lane_of(rows[p], 8 * p + k) for k in range(8)]
        a = {(i, k): wide(own[k][i : i + 1, :]) for k in range(8) for i in range(k, 8)}
        col = [lane_of(rows[p + 1], 8 * p + k) for k in range(8)] if p < 7 else None
        out = None
        for k in range(8):
            inverse = 1.0 / a[k, k]
            for j in range(k + 1, 8):
                factor = a[j, k] * inverse
                for i in range(j, 8):
                    a[i, j] = a[i, j] - a[i, k] * factor
                row[j] = row[j] - factor * row[k]
                if col:
                    col[j] = col[j] - factor * col[k]
            if col:
                rows[p + 1] = rows[p + 1] - col[k] * (row[k] * inverse)
            final = row[k] * lax.rsqrt(a[k, k])
            out = final if out is None else jnp.where(sub == k, final, out)
        outs.append(out)
        if p < 6:
            high = out.astype(BF16).astype(F32)
            low = out - high
            left = jnp.concatenate([high, high, low], axis=0)[:, :BLOCK].astype(BF16)
            right = jnp.concatenate([high, low, high], axis=0).astype(BF16)
            update = lax.dot_general(left, right, (((0,), (0,)), ((), ())), preferred_element_type=F32)
            for i in range(p + 2, 8):
                rows[i] = rows[i] - update[8 * i : 8 * i + 8]
    return outs


def cholesky_inverse(g, x, done, beside, before_last):
    lane = lax.broadcasted_iota(jnp.int32, (8, LANES), 1)
    sub = lax.broadcasted_iota(jnp.int32, (8, LANES), 0)

    def step(index, last=False):
        rows = [
            jnp.where(
                lane < BLOCK,
                g[8 * i : 8 * i + 8, :LANES],
                jnp.where(lane - BLOCK == sub + 8 * i, 1.0, 0.0),
            )
            for i in range(8)
        ]
        block = jnp.concatenate(factor_block(rows), axis=0)
        inverse = split(block[:, BLOCK:])
        solved = stack3(inverse, split(x[:BLOCK, :]), (1, 0))
        if last:
            done[S - BLOCK :, :] = solved
            return
        done[pl.ds(pl.multiple_of(index * BLOCK, BLOCK), BLOCK), :] = solved
        upper = stack3(inverse, split(g[:BLOCK, :]), (1, 0))
        rest = split(upper[:, BLOCK:])
        g[: S - BLOCK, : S - BLOCK] = g[BLOCK:, BLOCK:] - stack3(rest, rest, (0, 0))
        x[: S - BLOCK, :] = x[BLOCK:, :] - stack3(rest, split(solved), (0, 0))

    def loop(index, carry):
        beside(index)
        step(index)
        return carry

    lax.fori_loop(0, S // BLOCK - 1, loop, 0)
    before_last()
    step(S // BLOCK - 1, last=True)


def kernel(
    d_hbm, rs_hbm, w_hbm, cs_hbm, w2_hbm, ranks_hbm, out_ref,
    w_ref, w2_ref, ranks_ref,
    d_own, d_sib, d_high, d_low, w_own, w_sib, rst, rst_high, rst_low, regrouped, cs_ref,
    chunks, parts, sums, ys, ys_sib, y_high, y_low, cs_high, cs_low, w2_col,
    g, pc, projected, mixed_in, mixed_out, own_pair, xi, winv, bt_out, bt_in, bt_all, bt, first_sum,
    g_out, g_in, g_all,
    in_sem, sib_sem, gather_recv, gather_send, pass_send, pass_recv,
    z_send, z_recv, re_send, re_recv, b_send, b_recv, own_sem, g_send, g_recv, reach_sem,
):
    fiber, me = lax.axis_index("fiber"), lax.axis_index("row")
    z, core = lax.div(fiber, 2), lax.rem(fiber, 2)
    x, y = lax.div(me, SIDE), lax.rem(me, SIDE)
    other = 1 - core
    sibling = (2 * z + other, me)
    closing = []

    def at(dx, dy):
        return lax.rem(x + dx + SIDE, SIDE) * SIDE + lax.rem(y + dy + SIDE, SIDE)

    def z_peer(distance):
        return lax.rem(z + distance, CHIPS)

    def remote(src, dst, send, recv, device):
        copy = pltpu.make_async_remote_copy(
            src_ref=src, dst_ref=dst, send_sem=send, recv_sem=recv, device_id=device, device_id_type=MESH
        )
        copy.start()
        return copy

    def wait_bytes(ref, sem):
        pltpu.make_async_copy(ref, ref, sem).wait()

    def fetch(src, dst, i):
        copy = pltpu.make_async_copy(src, dst, in_sem.at[i])
        copy.start()
        return copy

    half_of_core = pl.ds(pl.multiple_of(core * HALF, HALF), HALF)
    half_of_sibling = pl.ds(pl.multiple_of(other * HALF, HALF), HALF)
    fetch_rs = fetch(rs_hbm.at[half_of_core], rst.at[me], 0)
    fetch_d = fetch(d_hbm.at[0], d_own, 1)
    fetch_cs = fetch(cs_hbm, cs_ref, 2)
    fetch_w = fetch(w_hbm, w_ref, 3)
    fetch_later = [fetch(w2_hbm, w2_ref, 4), fetch(ranks_hbm, ranks_ref, 5)]
    peers = [(fiber, at(dx, dy)) for dx, dy in OTHERS]
    peers += [(2 * z_peer(e) + core, me) for e in (1, CHIPS - 1)]
    peers += [sibling]
    barrier = pltpu.get_barrier_semaphore()
    for peer in peers:
        pl.semaphore_signal(barrier, inc=1, device_id=peer, device_id_type=MESH)
    fetch_w.wait()
    w_t = jnp.broadcast_to(w_ref[...], (LANES, S)).T
    w_own[0], w_own[1] = w_t[:HALF], w_t[HALF:]
    fetch_rs.wait()
    fetch_d.wait()
    pl.semaphore_wait(barrier, len(peers))

    def reach(step):
        if step > 0:
            pl.semaphore_wait(reach_sem.at[step - 1], 2)
        if step < 3:
            for e in (2**step, CHIPS - 2**step):
                to = (2 * z_peer(e) + core, me)
                pl.semaphore_signal(reach_sem.at[step], inc=1, device_id=to, device_id_type=MESH)

    def drain():
        while closing:
            closing.pop(0)()

    reach(0)

    def gather(buf, which):
        send = gather_send.at[which]
        closing.append(lambda: wait_bytes(rst.at[pl.ds(0, ROWS - 1)], send))

        def piece(s, slot):
            return buf(slot, s * SUB, SUB)

        def receive(s, j, d):
            if which == 1 and j > 0:
                return gather_recv.at[1, 0, 1, 0]
            return gather_recv.at[which, s, j, d - 1]

        def push(s, slot, axis, j):
            for d in (2, 1, 3):
                ref = piece(s, slot)
                to = at(d, 0) if axis == 0 else at(0, d)
                remote(ref, ref, send, receive(s, j, d), (fiber, to))

        def arrived(s, ex, ey):
            near, last = (ex, ey) if s == 0 else (ey, ex)
            sem = receive(s, 1 + near, last) if last else receive(s, 0, near)
            slot = at(-ex, -ey)
            wait_bytes(piece(s, slot), sem)
            if not last:
                push(s, slot, 1 - s, 1 + near)

        def start():
            for s in range(2):
                push(s, me, s, 0)
            for s in range(2):
                push(s, me, 1 - s, 1)

        def first():
            for e in (1, 3, 2):
                for s in range(2):
                    arrived(s, *((e, 0) if s == 0 else (0, e)))

        def rest(offsets):
            if which == 1:
                wait_bytes(rst.at[pl.ds(0, ROWS - SIDE)], receive(0, 1, 1))
                return
            for ex, ey in offsets:
                for s in range(2):
                    if (ex, ey)[1 - s]:
                        arrived(s, ex, ey)

        return start, first, rest

    def add_to(ref, first, value):
        ref[...] = value if first == 0 else ref[...] + value

    def fiber_sum(value, which, beside):
        for i in range(CHIPS):
            chunks[which, i] = value[10 * i : 10 * i + 10]
        sent, got = z_send.at[which], z_recv.at[which]
        for e in AWAY:
            to = z_peer(e)
            remote(chunks.at[which, to], parts.at[which, z], sent.at[0], got.at[0], (2 * to + core, me))
        parts[which, z] = chunks[which, z]
        beside()
        wait_bytes(parts.at[which, pl.ds(0, CHIPS - 1)], got.at[0])
        total = parts[which, 0]
        for i in range(1, CHIPS):
            total = total + parts[which, i]
        sums[which, z] = total
        for e in AWAY:
            to = z_peer(e)
            remote(sums.at[which, z], sums.at[which, z], sent.at[1], got.at[1], (2 * to + core, me))
        for i in range(2):
            closing.append(lambda i=i: wait_bytes(parts.at[which, pl.ds(0, CHIPS - 1)], sent.at[i]))
        wait_bytes(sums.at[which, pl.ds(0, CHIPS - 1)], got.at[1])
        return jnp.concatenate([sums[which, i] for i in range(CHIPS)], axis=0)

    to_sibling = [
        remote(d_own, d_sib, sib_sem.at[0, 0], sib_sem.at[1, 0], sibling),
        remote(w_own.at[other], w_sib, sib_sem.at[0, 1], sib_sem.at[1, 1], sibling),
    ]
    for copy in to_sibling:
        closing.append(copy.wait_send)

    def columns(slot):
        return pl.ds(pl.multiple_of(slot * LANES, LANES), LANES)

    def first_group(first, slots):
        if first == 0:
            fetch_cs.wait()
            for copy in fetch_later:
                copy.wait()
            cs_high[...], cs_low[...] = split(cs_ref[...].T)
            w2_col[...] = jnp.broadcast_to(w2_ref[...], (LANES, S)).T
            for copy in to_sibling:
                copy.wait_recv()
            i = 0
            for offsets in GROUPS:
                for ex, ey in offsets:
                    cols = columns(at(-ex, -ey))
                    here = slice(i * LANES, (i + 1) * LANES)
                    d_high[:LANES, here], d_low[:LANES, here] = split(d_own[:, cols])
                    d_high[LANES:, here], d_low[LANES:, here] = split(d_sib[:, cols])
                    i += 1
        for i, slot in enumerate(slots):
            here = slice((first + i) * LANES, (first + i + 1) * LANES)
            rst_high[:, here], rst_low[:, here] = split(rst[slot])
        here = slice(first * LANES, (first + len(slots)) * LANES)
        add_to(
            first_sum, first, dot3((rst_high[:, here], rst_low[:, here]), (d_high[:, here], d_low[:, here]), (1, 1))
        )

    start, first, rest = gather(lambda slot, start, size: rst.at[slot, pl.ds(start, size)], 0)
    start()
    reach(1)
    first()
    reach(2)
    count = 0
    for offsets in GROUPS:
        rest(offsets)
        first_group(count, [at(-ex, -ey) for ex, ey in offsets])
        count += len(offsets)
    def regroup():
        for dx, dy in OTHERS:
            to = at(dx, dy)
            remote(d_own.at[:, columns(to)], regrouped.at[me], re_send, re_recv, (fiber, to))
        regrouped[me] = d_own[:, columns(me)]
        square = (S, S)
        identity = jnp.where(
            lax.broadcasted_iota(jnp.int32, square, 0) == lax.broadcasted_iota(jnp.int32, square, 1), 1.0, 0.0
        )
        g[...] = identity
        xi[0], xi[1] = identity, identity

    reach(3)
    one = fiber_sum(first_sum[:, :LANES] * w_own[core] + first_sum[:, LANES:] * w_sib[...], 0, regroup)
    closing.append(lambda: wait_bytes(regrouped.at[pl.ds(0, ROWS - 1)], re_send))

    def to_pair(value, which):
        own_pair[which, core] = value
        ref = own_pair.at[which, core]
        copy = remote(ref, ref, own_sem.at[0, which], own_sem.at[1, which], sibling)
        closing.append(copy.wait_send)
        copy.wait_recv()
        return own_pair[which].reshape(S, LANES)

    def gram_sum(block, which, beside):
        high, low = split(jnp.concatenate([block, jnp.zeros((LANES // 2, LANES), F32)], axis=0))
        for c, first in ((0, 0), (1, LANES)):

            @pl.when(core == c)
            def _():
                last = LANES if c == 0 else 3 * LANES
                part = stack3((high[first:last], low[first:last]), (high[first:], low[first:]), (1, 1))
                for i in range(ROWS):
                    strip = part[8 * i : 8 * i + 8]
                    if c == 0:
                        tiles = [strip[:, LANES * t : LANES * (t + 1)] for t in range(3)]
                    else:
                        tiles = [strip[:, :LANES], strip[:, LANES:], part[LANES + 8 * i : LANES + 8 * i + 8, LANES:]]
                    for t in range(3):
                        g_out[which, i, t] = tiles[t]

        for dx, dy in OTHERS:
            to = at(dx, dy)
            remote(g_out.at[which, to], g_in.at[which, me], g_send.at[which, 0], g_recv.at[which, 0], (fiber, to))
        g_in[which, me] = g_out[which, me]
        beside[0]()
        wait_bytes(g_in.at[which, pl.ds(0, ROWS - 1)], g_recv.at[which, 0])
        total = g_in[which, 0]
        for i in range(1, ROWS):
            total = total + g_in[which, i]
        g_all[which, core, me] = total
        ref = g_all.at[which, core, me]
        for dx, dy in OTHERS:
            to = at(dx, dy)
            remote(ref, ref, g_send.at[which, 1], g_recv.at[which, 1], (fiber, to))
            remote(ref, ref, g_send.at[which, 2], g_recv.at[which, 2], (2 * z + other, to))
        remote(ref, ref, g_send.at[which, 2], g_recv.at[which, 2], sibling)
        for i in range(2):
            closing.append(lambda i=i: wait_bytes(g_in.at[which, pl.ds(0, ROWS - 1)], g_send.at[which, i]))
        closing.append(lambda: wait_bytes(g_in.at[which], g_send.at[which, 2]))
        beside[1]()
        wait_bytes(g_all.at[which, core, pl.ds(0, ROWS - 1)], g_recv.at[which, 1])
        wait_bytes(g_all.at[which, other], g_recv.at[which, 2])
        for i in range(ROWS):
            strip, under = slice(8 * i, 8 * i + 8), slice(LANES + 8 * i, LANES + 8 * i + 8)
            g[strip, :LANES] = g_all[which, 0, i, 0]
            g[strip, LANES : 2 * LANES] = g_all[which, 0, i, 1]
            g[strip, 2 * LANES :] = g_all[which, 0, i, 2][:, : LANES // 2]
            g[under, LANES : 2 * LANES] = g_all[which, 1, i, 0]
            g[under, 2 * LANES :] = g_all[which, 1, i, 1][:, : LANES // 2]
            if i < ROWS // 2:
                g[2 * LANES + 8 * i : 2 * LANES + 8 * i + 8, 2 * LANES :] = g_all[which, 1, i, 2][:, : LANES // 2]

    block_one = to_pair(one, 0)
    ys[me] = one
    start, first, rest = gather(lambda slot, start, size: ys.at[slot, pl.ds(start, size)], 1)
    gram_sum(block_one, 0, (start, first))

    def pass_on(index):
        @pl.when(index == 1)
        def _():
            rest(None)
            remote(ys, ys_sib, pass_send, pass_recv, sibling)

    def project_one():
        wait_bytes(ys_sib, pass_recv)
        wait_bytes(regrouped.at[pl.ds(0, ROWS - 1)], re_recv)
        for j in range(ROWS):
            here = slice(j * LANES, (j + 1) * LANES)
            y_high[half_of_core, here], y_low[half_of_core, here] = split(ys[j])
            y_high[half_of_sibling, here], y_low[half_of_sibling, here] = split(ys_sib[j])
        slabs = split(regrouped[...].reshape(ROWS * LANES, LANES))
        projected[...] = dot3((y_high[...], y_low[...]), slabs, (1, 0))

    cholesky_inverse(g, xi.at[0], winv, pass_on, project_one)
    closing.append(lambda: wait_bytes(ys, pass_send))
    index = lax.broadcasted_iota(jnp.int32, (S, LANES), 0)
    pc[...] = jnp.where(index < ranks_ref[0], dot3(split(winv[...]), split(projected[...]), (1, 0)), 0.0)

    pc_pair = split(pc[...])
    mixed = dot3((cs_high[...], cs_low[...]), pc_pair, (1, 0)) * w2_col[...]
    mixed_out[0], mixed_out[1] = mixed[:HALF], mixed[HALF:]
    exchange = remote(mixed_out.at[other], mixed_in, sib_sem.at[0, 2], sib_sem.at[1, 2], sibling)
    closing.append(exchange.wait_send)
    exchange.wait_recv()
    block_two = to_pair(fiber_sum(mixed_out[core] + mixed_in[...], 1, drain), 1)

    def nothing():
        pass

    def project_two():
        drain()
        bt_part = dot3(split(block_two), pc_pair, (1, 1))
        for j in range(ROWS):
            bt_out[j] = bt_part[20 * j : 20 * j + 20]
        for dx, dy in OTHERS:
            to = at(dx, dy)
            remote(bt_out.at[to], bt_in.at[me], b_send.at[0], b_recv.at[0], (fiber, to))
        bt_in[me] = bt_out[me]


    gram_sum(block_two, 1, (nothing, project_two))
    def add_up(index):
        @pl.when(index == 2)
        def _():
            wait_bytes(bt_in.at[pl.ds(0, ROWS - 1)], b_recv.at[0])
            total = bt_in[0]
            for j in range(1, ROWS):
                total = total + bt_in[j]
            bt_all[me] = total
            for dx, dy in OTHERS:
                to = at(dx, dy)
                remote(bt_all.at[me], bt_all.at[me], b_send.at[1], b_recv.at[1], (fiber, to))

    def assemble():
        wait_bytes(bt_all.at[pl.ds(0, ROWS - 1)], b_recv.at[1])
        for j in range(ROWS):
            bt[20 * j : 20 * j + 20, :] = bt_all[j]

    cholesky_inverse(g, xi.at[1], winv, add_up, nothing)
    assemble()
    odd = lax.rem(me, 2)
    window = winv[pl.ds(pl.multiple_of(20 * me - 4 * odd, 8), 24), :]
    mine = jnp.where(odd == 0, window[:20], window[4:])
    keep = lax.broadcasted_iota(jnp.int32, mine.shape, 0) + 20 * me < ranks_ref[1]
    mine = jnp.where(keep, mine, 0.0)
    core_t = dot3(split(mine), split(bt[...]), (1, 0))
    for i in range(S // ROWS):
        out_ref[i] = core_t[i : i + 1]
    drain()
    for i in range(2):
        wait_bytes(bt_all.at[pl.ds(0, ROWS - 1)], b_send.at[i])


def local(deltas, row_sketch, slab_sketch, core_sketch, slab_sketch_two, ranks):
    vmem = lambda *shape: pltpu.VMEM(shape, F32)
    half = lambda *shape: pltpu.VMEM(shape, BF16)
    dma = pltpu.SemaphoreType.DMA
    in_hbm = pl.BlockSpec(memory_space=pltpu.HBM)
    core_t = pl.pallas_call(
        kernel,
        out_shape=jax.ShapeDtypeStruct((S // ROWS, 1, S), F32),
        in_specs=[in_hbm] * 6,
        out_specs=pl.BlockSpec(memory_space=pltpu.VMEM),
        scratch_shapes=[
            vmem(1, S), vmem(1, S), pltpu.SMEM((2,), jnp.int32),
            vmem(LANES, 2048), vmem(LANES, 2048),
            half(2 * LANES, 2048), half(2 * LANES, 2048),
            vmem(2, HALF, LANES), vmem(HALF, LANES),
            vmem(ROWS, HALF, LANES), half(HALF, 2048), half(HALF, 2048),
            vmem(ROWS, LANES, LANES), vmem(S, S),
            vmem(2, CHIPS, 10, LANES), vmem(2, CHIPS, 10, LANES), vmem(2, CHIPS, 10, LANES),
            vmem(ROWS, HALF, LANES), vmem(ROWS, HALF, LANES),
            half(S, 2048), half(S, 2048),
            half(S, S), half(S, S), vmem(S, LANES),
            vmem(S, S), vmem(S, LANES), vmem(S, LANES),
            vmem(HALF, LANES), vmem(2, HALF, LANES), vmem(2, 2, HALF, LANES),
            vmem(2, S, S), vmem(S, S),
            vmem(ROWS, 20, S), vmem(ROWS, 20, S), vmem(ROWS, 20, S), vmem(S, S),
            vmem(HALF, 2 * LANES),
            vmem(2, ROWS, 3, 8, LANES), vmem(2, ROWS, 3, 8, LANES), vmem(2, 2, ROWS, 3, 8, LANES),
            dma((6,)), dma((2, 3)),
            dma((2, 2, 5, 3)), dma((2,)),
            dma(()), dma(()),
            dma((2, 2)), dma((2, 2)),
            dma(()), dma(()),
            dma((2,)), dma((2,)),
            dma((2, 2)), dma((2, 3)), dma((2, 3)),
            pltpu.SemaphoreType.REGULAR((3,)),
        ],
        compiler_params=pltpu.CompilerParams(
            collective_id=0, has_side_effects=True, vmem_limit_bytes=62 * 2**20
        ),
        cost_estimate=pl.CostEstimate(flops=2 * 10**9, bytes_accessed=4 * 10**6, transcendentals=0),
    )(deltas, row_sketch.T, slab_sketch, core_sketch, slab_sketch_two, ranks)
    return jnp.transpose(core_t, (1, 2, 0))


def solution(mesh):
    in_specs = (
        P("fiber", "row", None),
        P("row", None),
        P("fiber", None),
        P(),
        P("fiber", None),
        P(),
    )
    out_specs = P("fiber", None, "row")
    return jax.shard_map(local, mesh=mesh, in_specs=in_specs, out_specs=out_specs, check_vma=False)
```
